256 devices in a mesh: dom: 32 (over x, y, core), spec: 8 (over z).
Axes of the slice: x: 4, y: 4, z: 8, core: 2. Of those that a mesh axis runs over, the one named last changes fastest.
Arguments:
- spectrum: float32 [1296, 32768], P('spec', 'dom'), may hold values from 0.2 to 2
- normals: float32 [2, 3, 65536], P(None, None, 'dom'), may hold values from -3 to 3, as said below
- conn: int32 [3, 65536], P(None, 'dom'), may hold values from 0 to 1535, as said below
- send_nodes: int32 [32, 4, 128], P('dom'), may hold values from 0 to 1023, as said below
- step_weight: float32 [32768], P('dom'), may hold values from 0.02 to 0.06
- group_speed: float32 [36], replicated, may hold values from 0.25 to 1
- dia_plus: int32 [1296], replicated, may hold values from 0 to 1295, as said below
- dia_minus: int32 [1296], replicated, may hold values from 0 to 1295, as said below
- dia_coeff: float32 [1296], replicated, may hold values from 0.01 to 0.04
Outputs:
- spectrum_out: float32 [1296, 32768], P(None, ('dom', 'spec'))
The draws below stay inside these ranges and needn't reach their ends.
Inputs may be any that keep to these rules, and one draw needn't show every extreme that they name: `conn`: for partition i, an entry below 1024 names an owned node; an entry 1024 + m * 128 + s names slot s of ghost block m, from partition i + g (g as in the reference program); only blocks of partitions that exist are named, and each block only in a leading run of its slots. `send_nodes`: each row lists distinct owned nodes of the sending partition. `dia_plus`: for bin f * 36 + d the partner has frequency min(f + 1 or f + 2, 35) and a direction 1 to 3 steps higher, modulo 36. `dia_minus`: for bin f * 36 + d the partner has frequency max(f - 1 or f - 2, 0) and a direction 1 to 3 steps lower, modulo 36. `normals`: for each triangle the three vectors sum to zero and no two are parallel.
All inputs are finite; a program needn't handle non-finite values.
Results may differ from the reference program's by a relative error of at most 0.00002.
Values sent between devices are 32-bit elements; how exact they have to be, the bound alone decides.
A program may use at most 64 MiB of HBM per device.

```python
import math
import jax
import jax.numpy as jnp
from jax import lax

NDIR = 36
NFREQ = 36
NODE_DEV = 1024
SLOT = 128
REACH = 2
STEPS = 2
BINS = 1296
ELEM_DEV = 2048
PARTITIONS = 32
NODES = 32768
ELEMENTS = 65536
N_DOM = 32


def draw_conn(key, part):
    blocks = 2 * REACH
    local_total = NODE_DEV + blocks * SLOT
    first_key, second_key = jax.random.split(jax.random.fold_in(key, 11))
    counts = jax.random.randint(first_key, (PARTITIONS, blocks), SLOT // 2, SLOT + 1)
    counts = counts.at[1, blocks - 1].set(SLOT)
    raw_index = jax.random.randint(second_key, (3, PARTITIONS, ELEM_DEV), 0, local_total)
    ghost_index = raw_index - NODE_DEV
    block_index = jnp.clip(ghost_index // SLOT, 0, blocks - 1)
    slot_index = ghost_index % SLOT
    offset = jnp.where(block_index < REACH, block_index - REACH, block_index - REACH + 1)
    part_of = jnp.arange(PARTITIONS, dtype=jnp.int32)[None, :, None]
    sender = part_of + offset
    limit = counts[jnp.broadcast_to(part_of, block_index.shape), block_index]
    usable = (sender >= 0) & (sender < PARTITIONS) & (slot_index < limit)
    local_index = jnp.where(ghost_index < 0, raw_index, jnp.where(usable, raw_index, raw_index % NODE_DEV))
    local_index = local_index.at[0, 0, 0].set(0)
    local_index = local_index.at[0, 1, 0].set(local_total - 1)
    return local_index.reshape(3, PARTITIONS * ELEM_DEV).astype(jnp.int32)


def draw_send_nodes(key, part):
    blocks = 2 * REACH
    keys = jax.random.split(jax.random.fold_in(key, 12), PARTITIONS * blocks)
    chosen = jax.vmap(lambda one_key: jax.random.permutation(one_key, NODE_DEV)[:SLOT])(keys)
    return chosen.reshape(PARTITIONS, blocks, SLOT).astype(jnp.int32)


def partner_bins(key, salt, upward):
    bins = jnp.arange(BINS, dtype=jnp.int32)
    freq = bins // NDIR
    direc = bins % NDIR
    freq_key, dir_key = jax.random.split(jax.random.fold_in(key, salt))
    freq_step = jax.random.randint(freq_key, (BINS,), 1, 3)
    dir_step = jax.random.randint(dir_key, (BINS,), 1, 4)
    if upward:
        new_freq = jnp.minimum(freq + freq_step, NFREQ - 1)
        new_dir = (direc + dir_step) % NDIR
    else:
        new_freq = jnp.maximum(freq - freq_step, 0)
        new_dir = (direc - dir_step) % NDIR
    return (new_freq * NDIR + new_dir).astype(jnp.int32)


def draw_dia_plus(key, part):
    return partner_bins(key, 13, True)


def draw_dia_minus(key, part):
    return partner_bins(key, 14, False)


def draw_normals(key, part):
    keys = jax.random.split(jax.random.fold_in(key, 15), 3)
    rotation = jax.random.uniform(keys[0], (ELEMENTS,), jnp.float32, -math.pi, math.pi)
    uniform_draw = jax.random.uniform(keys[1], (ELEMENTS,), jnp.float32)
    length = jnp.exp(math.log(0.5) + (math.log(2.0) - math.log(0.5)) * uniform_draw)
    jitter = jax.random.uniform(keys[2], (2, 2, ELEMENTS), jnp.float32, -0.1, 0.1)
    angles = rotation[None, :] + 2.0 * math.pi / 3.0 * jnp.arange(2, dtype=jnp.float32)[:, None]
    first_two = jnp.stack([jnp.cos(angles), jnp.sin(angles)]) + jitter
    third = -(first_two[:, 0] + first_two[:, 1])
    whole = jnp.concatenate([first_two, third[:, None, :]], axis=1)
    return (whole * length[None, None, :]).astype(jnp.float32)


def levels(stream_key, dims, shards, least, high):
    gain, own = 1.0, jax.random.fold_in(stream_key, 6)
    for position, parts in shards:
        heights = jnp.exp(jax.random.uniform(jax.random.fold_in(own, position), (parts,), jnp.float32, least / len(shards), high / len(shards)))
        gain = gain * jnp.repeat(heights, dims[position] // parts).reshape([-1 if axis == position else 1 for axis in range(len(dims))])
    return gain


def setup_inputs(seed: int = 0) -> dict:
    key_list = jax.random.split(jax.random.key(seed), 10)
    spectrum = jnp.clip(jnp.exp(math.log(2.0) - 2.3025851 * jax.random.uniform(key_list[0], (BINS, NODES), jnp.float32) ** levels(key_list[0], (BINS, NODES), ((0, 8), (1, 32)), -0.2, 0.2)), 0.2, 2.0)
    normals = draw_normals(jax.random.fold_in(key_list[9], 71), 0)
    conn = draw_conn(jax.random.fold_in(key_list[9], 71), 0)
    send_nodes = draw_send_nodes(jax.random.fold_in(key_list[9], 71), 0)
    step_weight = jnp.clip(0.02 + 0.04 * jax.random.uniform(key_list[4], (NODES,), jnp.float32) ** levels(key_list[4], (NODES,), ((0, 32),), -0.2, 0.2), 0.02, 0.06)
    group_speed = jnp.clip(jnp.exp(jax.random.uniform(key_list[5], (NFREQ,), jnp.float32, math.log(0.25), math.log(1.0))), 0.25, 1.0)
    dia_plus = draw_dia_plus(jax.random.fold_in(key_list[9], 71), 0)
    dia_minus = draw_dia_minus(jax.random.fold_in(key_list[9], 71), 0)
    dia_coeff = jnp.clip(jnp.exp(jax.random.uniform(key_list[8], (BINS,), jnp.float32, math.log(0.01), math.log(0.04))), 0.01, 0.04)
    return {"spectrum": spectrum, "normals": normals, "conn": conn, "send_nodes": send_nodes, "step_weight": step_weight, "group_speed": group_speed, "dia_plus": dia_plus, "dia_minus": dia_minus, "dia_coeff": dia_coeff}


weight_plus = 1.25 ** -4
weight_minus = 0.75 ** -4
weight_both = 0.9375 ** -4


def global_corners(conn, send_nodes):
    part_of = (jnp.arange(ELEMENTS, dtype=jnp.int32) // ELEM_DEV)[None, :]
    ghost_index = conn - NODE_DEV
    block_index = jnp.clip(ghost_index // SLOT, 0, 2 * REACH - 1)
    slot_index = ghost_index % SLOT
    offset = jnp.where(block_index < REACH, block_index - REACH, block_index - REACH + 1)
    sender = jnp.clip(part_of + offset, 0, N_DOM - 1)
    row_index = 2 * REACH - 1 - block_index
    remote = sender * NODE_DEV + send_nodes[sender, row_index, slot_index]
    return jnp.where(ghost_index < 0, part_of * NODE_DEV + conn, remote).astype(jnp.int32)


def residual_of(energy, corners, normals, speed_east, speed_north, node_count):
    coeffs = [speed_east[:, None] * normals[0, vertex][None, :] + speed_north[:, None] * normals[1, vertex][None, :] for vertex in range(3)]
    outward = [jnp.maximum(item, 0.0) for item in coeffs]
    inward = [jnp.minimum(item, 0.0) for item in coeffs]
    denom = inward[0] + inward[1] + inward[2]
    values = [jnp.take(energy, corners[vertex], axis=1) for vertex in range(3)]
    inflow = (inward[0] * values[0] + inward[1] * values[1] + inward[2] * values[2]) / denom
    totals = jnp.zeros((energy.shape[0], node_count), jnp.float32)
    for vertex in range(3):
        totals = totals.at[:, corners[vertex]].add(outward[vertex] * (values[vertex] - inflow))
    return totals


def interact(energy, dia_plus, dia_minus, dia_coeff):
    upper = jnp.take(energy, dia_plus, axis=0)
    lower = jnp.take(energy, dia_minus, axis=0)
    term = dia_coeff[:, None] * (energy * energy * (weight_plus * upper + weight_minus * lower) - 2.0 * weight_both * energy * upper * lower)
    change = (-2.0 * term).at[dia_plus].add(term).at[dia_minus].add(term)
    return energy + change


def reference(spectrum, normals, conn, send_nodes, step_weight, group_speed, dia_plus, dia_minus, dia_coeff):
    corners = global_corners(conn, send_nodes)
    directions = jnp.arange(NDIR, dtype=jnp.int32).astype(jnp.float32) * (2.0 * math.pi / NDIR)

    def one_frequency(inputs):
        freq_index, freq_block = inputs
        speed = group_speed[freq_index]
        speed_east = speed * jnp.cos(directions)
        speed_north = speed * jnp.sin(directions)
        energy = freq_block
        for sweep_index in range(STEPS):
            energy = energy - step_weight[None, :] * residual_of(energy, corners, normals, speed_east, speed_north, NODES)
        return energy

    propagated = lax.map(one_frequency, (jnp.arange(NFREQ, dtype=jnp.int32), spectrum.reshape(NFREQ, NDIR, NODES)))
    by_part = jnp.transpose(propagated.reshape(BINS, N_DOM, NODE_DEV), (1, 0, 2))
    mixed = lax.map(lambda slab: interact(slab, dia_plus, dia_minus, dia_coeff), by_part)
    return jnp.transpose(mixed, (1, 0, 2)).reshape(BINS, NODES)
```

```python
import functools
import math

import jax
import jax.numpy as jnp
import numpy as np
from jax import lax
from jax.experimental import pallas as pl
from jax.experimental.pallas import tpu as pltpu
from jax.sharding import PartitionSpec as P

NDIR = 36
NFREQ = 36
BINS = NDIR * NFREQ
STEPS = 2
DOM = 32
SPEC = 8
ROWS = BINS // SPEC
PAD = 168
MAIN = 160
BOTH = 2 * PAD
OWN = 1024
SLOT = 128
BLOCKS = 4
EXT = OWN + BLOCKS * SLOT
ELEM = 2048
CHUNK = 256
CHUNKS = ELEM // CHUNK
TROWS = 88
OFFSETS = (-2, -1, 1, 2)
STRIDE = 48
LEAD = 8
PADDED = (NFREQ + 4) * STRIDE + 8

weight_plus = 1.25 ** (-4)
weight_minus = 0.75 ** (-4)
weight_both = 0.9375 ** (-4)

MESH = pl.DeviceIdType.MESH
f32, bf16 = jnp.float32, jnp.bfloat16


def split(value):
    high = value.astype(bf16).astype(f32)
    low = value - high
    return jnp.concatenate([high[:MAIN], low[:MAIN], high[MAIN:], low[MAIN:]], axis=0).astype(bf16)


def join(value):
    return jnp.concatenate(
        [
            value[:MAIN] + value[MAIN : 2 * MAIN],
            value[2 * MAIN : MAIN + PAD] + value[MAIN + PAD :],
        ],
        axis=0,
    )


def dot(left, right):
    return jnp.dot(left, right, preferred_element_type=f32)


def dot_t(left, right):
    return lax.dot_general(left, right, (((1,), (1,)), ((), ())), preferred_element_type=f32)


def lanes(index, size):
    return pl.ds(pl.multiple_of(index * size, size), size)


def kernel(
    spectrum,
    normals,
    conn,
    send_nodes,
    step_weight,
    group_speed,
    dia_plus,
    dia_minus,
    dia_coeff,
    table,
    out,
    energy,
    parts,
    send_hot,
    corner_hot,
    edge_hot,
    edge_weight,
    edge_diff,
    flux,
    own_sum,
    ghost_out,
    ghost_in,
    back_out,
    back_in,
    landing,
    linear,
    padded,
    term,
    code_plus,
    code_minus,
    coeff,
    halo_send,
    halo_recv,
    spec_send,
    spec_recv,
):
    dom = lax.axis_index("dom")
    spec = lax.axis_index("spec")

    barrier = pltpu.get_barrier_semaphore()
    for offset in OFFSETS:
        pl.semaphore_signal(
            barrier,
            inc=1,
            device_id={"dom": lax.rem(dom + offset + DOM, DOM), "spec": spec},
            device_id_type=MESH,
        )
    for shift in range(1, SPEC):
        pl.semaphore_signal(
            barrier,
            inc=1,
            device_id={"dom": dom, "spec": lax.rem(spec + shift, SPEC)},
            device_id_type=MESH,
        )

    for chunk in range(SPEC):
        energy[chunk, :ROWS] = spectrum[:, chunk * 128 : (chunk + 1) * 128]
        energy[chunk, ROWS:] = jnp.zeros((PAD - ROWS, 128), f32)
        parts[:, chunk * 128 : (chunk + 1) * 128] = split(energy[chunk])

    def hot_rows(rows, index, first=0):
        index = jnp.broadcast_to(index.astype(jnp.int16), (rows, index.shape[1]))
        row = lax.broadcasted_iota(jnp.int16, index.shape, 0) + jnp.int16(first)
        return jnp.where(row == index, bf16(1), bf16(0))

    for row in range(BLOCKS):
        send_hot[:, row * SLOT : (row + 1) * SLOT] = hot_rows(OWN, send_nodes[0, row : row + 1, :])

    pl.semaphore_wait(barrier, BLOCKS + SPEC - 1)

    def ghost_copy(step, row):
        return pltpu.make_async_remote_copy(
            src_ref=ghost_out.at[step, row],
            dst_ref=ghost_in.at[step, BLOCKS - 1 - row],
            send_sem=halo_send.at[step, 0, row],
            recv_sem=halo_recv.at[step, 0, row],
            device_id={"dom": lax.rem(dom + OFFSETS[row] + DOM, DOM), "spec": spec},
            device_id_type=MESH,
        )

    def back_copy(step, block):
        return pltpu.make_async_remote_copy(
            src_ref=back_out.at[step, block],
            dst_ref=back_in.at[step, BLOCKS - 1 - block],
            send_sem=halo_send.at[step, 1, block],
            recv_sem=halo_recv.at[step, 1, block],
            device_id={"dom": lax.rem(dom + OFFSETS[block] + DOM, DOM), "spec": spec},
            device_id_type=MESH,
        )

    def send_ghosts(step):
        pieces = join(dot(parts[:, :OWN], send_hot[...]))
        for row in range(BLOCKS):
            ghost_out[step, row] = pieces[:, row * SLOT : (row + 1) * SLOT]
            ghost_copy(step, row).start()

    def edge_weights(chunk, carry):
        parity = lax.rem(spec, 2) == 0
        east = jnp.where(parity, table[0], table[2])
        north = jnp.where(parity, table[1], table[3])
        at = lanes(chunk, 128)
        k = [
            east * normals[corner, 0:1, at] + north * normals[corner, 1:2, at]
            for corner in range(3)
        ]
        into = [jnp.maximum(value, 0.0) for value in k]
        away = [jnp.maximum(-value, 0.0) for value in k]
        for edge in range(3):
            a, b = edge, (edge + 1) % 3
            edge_weight[edge, :, at] = jnp.minimum(into[a], away[b]) - jnp.minimum(into[b], away[a])
        return carry

    def build_hot(chunk, carry):
        hot = []
        for corner in range(3):
            value = hot_rows(EXT, conn[corner : corner + 1, lanes(chunk, CHUNK)])
            corner_hot[:, lanes(chunk * 3 + corner, CHUNK)] = value
            hot.append(value)
        edge_hot[:, lanes(chunk * 2, CHUNK)] = hot[0] - hot[1]
        edge_hot[:, lanes(chunk * 2 + 1, CHUNK)] = hot[1] - hot[2]
        return carry

    def fluxes(chunk):
        at = lanes(chunk, CHUNK)

        def block(rows, low_rows):
            size = rows.stop - rows.start
            first = rows.start % (2 * NDIR)
            d01 = edge_diff[rows, :CHUNK] + edge_diff[low_rows, :CHUNK]
            d12 = edge_diff[rows, CHUNK:] + edge_diff[low_rows, CHUNK:]
            d20 = -(d01 + d12)
            w01, w12, w20 = [edge_weight[edge, first : first + size, at] for edge in range(3)]
            return [
                jnp.maximum(w01, 0.0) * d01 + jnp.minimum(w20, 0.0) * d20,
                jnp.maximum(w12, 0.0) * d12 + jnp.minimum(w01, 0.0) * d01,
                jnp.maximum(w20, 0.0) * d20 + jnp.minimum(w12, 0.0) * d12,
            ]

        for first in range(0, MAIN, 16):
            rows, low_rows = slice(first, first + 16), slice(MAIN + first, MAIN + first + 16)
            for corner, value in enumerate(block(rows, low_rows)):
                high = value.astype(bf16)
                column = lanes(chunk * 3 + corner, CHUNK)
                flux[rows, column] = high
                flux[low_rows, column] = (value - high.astype(f32)).astype(bf16)
        size = PAD - MAIN
        first = MAIN % (2 * NDIR)
        rows, low_rows = slice(2 * MAIN, 2 * MAIN + size), slice(2 * MAIN + size, BOTH)
        d01 = edge_diff[rows, :CHUNK] + edge_diff[low_rows, :CHUNK]
        d12 = edge_diff[rows, CHUNK:] + edge_diff[low_rows, CHUNK:]
        d20 = -(d01 + d12)
        w01, w12, w20 = [edge_weight[edge, first : first + size, at] for edge in range(3)]
        values = [
            jnp.maximum(w01, 0.0) * d01 + jnp.minimum(w20, 0.0) * d20,
            jnp.maximum(w12, 0.0) * d12 + jnp.minimum(w01, 0.0) * d01,
            jnp.maximum(w20, 0.0) * d20 + jnp.minimum(w12, 0.0) * d12,
        ]
        for corner, value in enumerate(values):
            high = value.astype(bf16).astype(f32)
            column = lanes(chunk * 3 + corner, CHUNK)
            flux[2 * MAIN :, column] = jnp.concatenate([high, value - high], axis=0).astype(bf16)

    def sweep(chunk, carry):
        edge_diff[...] = dot(parts[...], edge_hot[:, lanes(chunk, 2 * CHUNK)])
        fluxes(chunk)
        return carry

    first_bin = spec * ROWS
    first_freq = first_bin // NDIR
    row = lax.broadcasted_iota(jnp.int32, (PAD, 128), 0) + (first_bin - first_freq * NDIR)
    speed = jnp.full((PAD, 128), group_speed[first_freq], f32)
    for later in range(1, 6):
        value = group_speed[jnp.minimum(first_freq + later, NFREQ - 1)]
        speed = jnp.where(row >= later * NDIR, value, speed)

    send_ghosts(0)
    lax.fori_loop(0, CHUNKS, build_hot, 0)
    lax.fori_loop(0, ELEM // 128, edge_weights, 0)

    for step in range(STEPS):
        for block in range(BLOCKS):
            ghost_copy(step, BLOCKS - 1 - block).wait_recv()
            parts[:, OWN + block * SLOT : OWN + (block + 1) * SLOT] = split(ghost_in[step, block])
        lax.fori_loop(0, CHUNKS, sweep, 0)
        ghost_sum = join(dot_t(flux[...], corner_hot[OWN:, :]))
        for block in range(BLOCKS):
            back_out[step, block] = ghost_sum[:, block * SLOT : (block + 1) * SLOT]
            back_copy(step, block).start()

        def own_part(half, carry):
            rows = lanes(half, 512)
            own_sum[:, rows] = join(dot_t(flux[...], corner_hot[rows, :]))
            return carry

        lax.fori_loop(0, 2, own_part, 0)
        for block in range(BLOCKS):
            back_copy(step, block).wait_recv()
        returned = [split(back_in[step, row]) for row in range(BLOCKS)]
        returned = jnp.concatenate(returned, axis=1)
        for half in range(2):
            at = slice(half * 512, (half + 1) * 512)
            total = own_sum[:, at] + join(dot_t(returned, send_hot[at, :]))
            for quarter in range(4):
                chunk = half * 4 + quarter
                weight = step_weight[:, chunk * 128 : (chunk + 1) * 128]
                value = energy[chunk] - (speed * weight) * total[:, quarter * 128 : (quarter + 1) * 128]
                energy[chunk] = value
                if step + 1 < STEPS:
                    parts[:, chunk * 128 : (chunk + 1) * 128] = split(value)
        if step + 1 < STEPS:
            send_ghosts(step + 1)

    def spec_copy(shift):
        to = lax.rem(spec + shift, SPEC)
        return pltpu.make_async_remote_copy(
            src_ref=energy.at[to],
            dst_ref=landing.at[spec],
            send_sem=spec_send.at[shift - 1],
            recv_sem=spec_recv.at[shift - 1],
            device_id={"dom": dom, "spec": to},
            device_id_type=MESH,
        )

    for shift in (4, 3, 5, 2, 6, 1, 7):
        spec_copy(shift).start()
    landing[spec] = energy[spec]

    bin_ = lax.broadcasted_iota(jnp.int32, (1, BINS), 1).astype(f32)
    freq = jnp.floor((bin_ + 0.5) * (1.0 / NDIR))
    direction = bin_ - NDIR * freq

    def partner_code(partner, sign):
        partner = partner.astype(f32)
        other = jnp.floor((partner + 0.5) * (1.0 / NDIR))
        turn = sign * ((partner - NDIR * other) - direction)
        turn = jnp.where(turn < 0, turn + NDIR, turn)
        return 4 * jnp.maximum(sign * (other - freq), 1.0) + turn

    def to_column(value):
        for first in range(0, BINS, 128):
            size = min(128, BINS - first)
            piece = value[:, first : first + size]
            if size < 128:
                piece = jnp.concatenate([piece, jnp.zeros((1, 128 - size), f32)], axis=1)
            linear[first : first + size] = jnp.broadcast_to(piece, (128, 128)).T[:size]

    def to_padded(target):
        def one(f, carry):
            base = pl.multiple_of((f + 2) * STRIDE, 8)
            value = linear[pl.ds(f * NDIR, NDIR)]
            target[pl.ds(base + LEAD, NDIR)] = value
            target[pl.ds(base + LEAD - 3, 3)] = value[NDIR - 3 :]
            target[pl.ds(base + LEAD + NDIR, 3)] = value[:3]
            return carry

        lax.fori_loop(0, NFREQ, one, 0)

    for target, value in (
        (code_plus, partner_code(dia_plus[...], 1.0)),
        (code_minus, partner_code(dia_minus[...], -1.0)),
        (coeff, dia_coeff[...]),
    ):
        target[...] = jnp.zeros((PADDED, 128), f32)
        to_column(value)
        to_padded(target)

    for shift in range(1, SPEC):
        source = lax.rem(spec + SPEC - shift, SPEC)
        pltpu.make_async_remote_copy(
            src_ref=landing.at[source],
            dst_ref=landing.at[source],
            send_sem=spec_send.at[shift - 1],
            recv_sem=spec_recv.at[shift - 1],
            device_id={"dom": dom, "spec": source},
            device_id_type=MESH,
        ).wait_recv()

    half = NDIR // 2
    for source in range(SPEC):
        for piece in range(ROWS // half):
            f, second = divmod(source * (ROWS // half) + piece, 2)
            base = (f + 2) * STRIDE + LEAD
            value = landing[source, piece * half : (piece + 1) * half]
            padded[base + second * half : base + (second + 1) * half] = value
            if second:
                padded[base - 3 : base] = value[half - 3 :]
            else:
                padded[base + NDIR : base + NDIR + 3] = value[:3]
    for block in range(2):
        padded[block * STRIDE : (block + 1) * STRIDE] = padded[2 * STRIDE : 3 * STRIDE]
        last = (NFREQ + 2 + block) * STRIDE
        padded[last : last + STRIDE] = padded[(NFREQ + 1) * STRIDE : (NFREQ + 2) * STRIDE]

    wide = 40
    shifts = [(by, turn) for by in (1, 2) for turn in (1, 2, 3)]

    def terms(f, carry):
        base = pl.multiple_of((f + 2) * STRIDE + LEAD, 8)
        here = padded[pl.ds(base, wide)]
        plus = code_plus[pl.ds(base, wide)]
        minus = code_minus[pl.ds(base, wide)]
        upper = padded[pl.ds(base + STRIDE + 1, wide)]
        lower = padded[pl.ds(base - STRIDE - 1, wide)]
        for by, turn in shifts[1:]:
            code = float(4 * by + turn)
            upper = jnp.where(plus == code, padded[pl.ds(base + by * STRIDE + turn, wide)], upper)
            lower = jnp.where(minus == code, padded[pl.ds(base - by * STRIDE - turn, wide)], lower)
        value = coeff[pl.ds(base, wide)] * (
            here * here * (weight_plus * upper + weight_minus * lower)
            - 2.0 * weight_both * here * upper * lower
        )
        term[pl.ds(base, NDIR)] = value[:NDIR]
        term[pl.ds(base - 3, 3)] = value[NDIR - 3 : NDIR]
        term[pl.ds(base + NDIR, 3)] = value[:3]
        return carry

    lax.fori_loop(0, NFREQ, terms, 0)

    def gained(codes, at, code):
        rows = pl.ds(at, wide)
        return jnp.where(codes[rows] == code, term[rows], 0.0)

    def changes(f, carry):
        base = pl.multiple_of((f + 2) * STRIDE + LEAD, 8)
        value = padded[pl.ds(base, wide)] - 2.0 * term[pl.ds(base, wide)]
        for by, turn in shifts:
            code = float(4 * by + turn)
            value = value + gained(code_plus, base - by * STRIDE - turn, code)
            value = value + gained(code_minus, base + by * STRIDE + turn, code)
        out[pl.ds(f * NDIR, NDIR)] = value[:NDIR]
        return carry

    lax.fori_loop(0, NFREQ, changes, 0)
    high = (NFREQ + 1) * STRIDE + LEAD
    low = 2 * STRIDE + LEAD
    for turn in (1, 2, 3):
        code = float(4 + turn)
        out[BINS - NDIR :] = out[BINS - NDIR :] + gained(code_plus, high - turn, code)[:NDIR]
        out[:NDIR] = out[:NDIR] + gained(code_minus, low + turn, code)[:NDIR]

    for step in range(STEPS):
        for row in range(BLOCKS):
            ghost_copy(step, row).wait_send()
            back_copy(step, row).wait_send()
    for shift in range(1, SPEC):
        spec_copy(shift).wait_send()


def direction_table():
    rows = np.arange(TROWS)
    values = []
    for start in (0, NDIR // 2):
        angle = ((rows + start) % NDIR) * (2.0 * math.pi / NDIR)
        values += [np.cos(angle), np.sin(angle)]
    return np.repeat(np.stack(values)[:, :, None], 128, axis=2).astype(np.float32)


def on_device(
    spectrum, normals, conn, send_nodes, step_weight, group_speed, dia_plus, dia_minus, dia_coeff
):
    vmem = pl.BlockSpec(memory_space=pltpu.VMEM)
    smem = pl.BlockSpec(memory_space=pltpu.SMEM)
    return pl.pallas_call(
        kernel,
        out_shape=jax.ShapeDtypeStruct((BINS, SLOT), f32),
        in_specs=[vmem, vmem, vmem, vmem, vmem, smem, vmem, vmem, vmem, vmem],
        out_specs=vmem,
        scratch_shapes=[
            pltpu.VMEM((SPEC, PAD, 128), f32),
            pltpu.VMEM((BOTH, EXT), bf16),
            pltpu.VMEM((OWN, BLOCKS * SLOT), bf16),
            pltpu.VMEM((EXT, 3 * ELEM), bf16),
            pltpu.VMEM((EXT, 2 * ELEM), bf16),
            pltpu.VMEM((3, TROWS, ELEM), f32),
            pltpu.VMEM((BOTH, 2 * CHUNK), f32),
            pltpu.VMEM((BOTH, 3 * ELEM), bf16),
            pltpu.VMEM((PAD, OWN), f32),
            pltpu.VMEM((STEPS, BLOCKS, PAD, SLOT), f32),
            pltpu.VMEM((STEPS, BLOCKS, PAD, SLOT), f32),
            pltpu.VMEM((STEPS, BLOCKS, PAD, SLOT), f32),
            pltpu.VMEM((STEPS, BLOCKS, PAD, SLOT), f32),
            pltpu.VMEM((SPEC, PAD, 128), f32),
            pltpu.VMEM((BINS + 8, 128), f32),
            pltpu.VMEM((PADDED, 128), f32),
            pltpu.VMEM((PADDED, 128), f32),
            pltpu.VMEM((PADDED, 128), f32),
            pltpu.VMEM((PADDED, 128), f32),
            pltpu.VMEM((PADDED, 128), f32),
            pltpu.SemaphoreType.DMA((STEPS, 2, BLOCKS)),
            pltpu.SemaphoreType.DMA((STEPS, 2, BLOCKS)),
            pltpu.SemaphoreType.DMA((SPEC - 1,)),
            pltpu.SemaphoreType.DMA((SPEC - 1,)),
        ],
        compiler_params=pltpu.CompilerParams(
            collective_id=0, has_side_effects=True, vmem_limit_bytes=62 * 2**20
        ),
    )(
        spectrum,
        jnp.transpose(normals, (1, 0, 2)),
        conn,
        send_nodes,
        step_weight[None, :],
        group_speed,
        dia_plus[None, :],
        dia_minus[None, :],
        dia_coeff[None, :],
        jnp.asarray(direction_table()),
    )


def solution(mesh):
    in_specs = (
        P("spec", "dom"),
        P(None, None, "dom"),
        P(None, "dom"),
        P("dom", None, None),
        P("dom"),
        P(),
        P(),
        P(),
        P(),
    )
    out_specs = P(None, ("dom", "spec"))
    return jax.shard_map(
        on_device, mesh=mesh, in_specs=in_specs, out_specs=out_specs, check_vma=False
    )
```

```python
import functools
import math

import jax
import jax.numpy as jnp
import numpy as np
from jax import lax
from jax.experimental import pallas as pl
from jax.experimental.pallas import tpu as pltpu
from jax.sharding import PartitionSpec as P

NDIR = 36
NFREQ = 36
BINS = NDIR * NFREQ
STEPS = 2
DOM = 32
SPEC = 8
ROWS = BINS // SPEC
PAD = 168
MAIN = 160
BOTH = 2 * PAD
OWN = 1024
SLOT = 128
BLOCKS = 4
EXT = OWN + BLOCKS * SLOT
ELEM = 2048
CHUNK = 256
CHUNKS = ELEM // CHUNK
TROWS = 88
OFFSETS = (-2, -1, 1, 2)
STRIDE = 48
LEAD = 8
PADDED = (NFREQ + 4) * STRIDE + 8

weight_plus = 1.25 ** (-4)
weight_minus = 0.75 ** (-4)
weight_both = 0.9375 ** (-4)

MESH = pl.DeviceIdType.MESH
f32, bf16 = jnp.float32, jnp.bfloat16


def split(value):
    high = value.astype(bf16).astype(f32)
    low = value - high
    return jnp.concatenate([high[:MAIN], low[:MAIN], high[MAIN:], low[MAIN:]], axis=0).astype(bf16)


def join(value):
    return jnp.concatenate(
        [
            value[:MAIN] + value[MAIN : 2 * MAIN],
            value[2 * MAIN : MAIN + PAD] + value[MAIN + PAD :],
        ],
        axis=0,
    )


def dot(left, right):
    return jnp.dot(left, right, preferred_element_type=f32)


def dot_t(left, right):
    return lax.dot_general(left, right, (((1,), (1,)), ((), ())), preferred_element_type=f32)


def lanes(index, size):
    return pl.ds(pl.multiple_of(index * size, size), size)


def kernel(
    spectrum,
    normals,
    conn,
    send_nodes,
    step_weight,
    group_speed,
    dia_plus,
    dia_minus,
    dia_coeff,
    table,
    out,
    energy,
    parts,
    send_hot,
    corner_hot,
    edge_hot,
    edge_weight,
    own_diff,
    even_diff,
    odd_diff,
    flux,
    own_sum,
    ghost_out,
    ghost_in,
    back_out,
    back_in,
    landing,
    linear,
    padded,
    term,
    code_plus,
    code_minus,
    coeff,
    halo_send,
    halo_recv,
    spec_send,
    spec_recv,
):
    dom = lax.axis_index("dom")
    spec = lax.axis_index("spec")

    barrier = pltpu.get_barrier_semaphore()
    for offset in OFFSETS:
        pl.semaphore_signal(
            barrier,
            inc=1,
            device_id={"dom": lax.rem(dom + offset + DOM, DOM), "spec": spec},
            device_id_type=MESH,
        )
    for shift in range(1, SPEC):
        pl.semaphore_signal(
            barrier,
            inc=1,
            device_id={"dom": dom, "spec": lax.rem(spec + shift, SPEC)},
            device_id_type=MESH,
        )

    for chunk in range(SPEC):
        energy[chunk, :ROWS] = spectrum[:, chunk * 128 : (chunk + 1) * 128]
        energy[chunk, ROWS:] = jnp.zeros((PAD - ROWS, 128), f32)
        parts[:, chunk * 128 : (chunk + 1) * 128] = split(energy[chunk])

    def hot_rows(rows, index, first=0):
        index = jnp.broadcast_to(index.astype(jnp.int16), (rows, index.shape[1]))
        row = lax.broadcasted_iota(jnp.int16, index.shape, 0) + jnp.int16(first)
        return jnp.where(row == index, bf16(1), bf16(0))

    for row in range(BLOCKS):
        send_hot[:, row * SLOT : (row + 1) * SLOT] = hot_rows(OWN, send_nodes[0, row : row + 1, :])

    def ghost_copy(step, row):
        return pltpu.make_async_remote_copy(
            src_ref=ghost_out.at[step, row],
            dst_ref=ghost_in.at[step, BLOCKS - 1 - row],
            send_sem=halo_send.at[step, 0, row],
            recv_sem=halo_recv.at[step, 0, row],
            device_id={"dom": lax.rem(dom + OFFSETS[row] + DOM, DOM), "spec": spec},
            device_id_type=MESH,
        )

    def back_copy(step, block):
        return pltpu.make_async_remote_copy(
            src_ref=back_out.at[step, block],
            dst_ref=back_in.at[step, BLOCKS - 1 - block],
            send_sem=halo_send.at[step, 1, block],
            recv_sem=halo_recv.at[step, 1, block],
            device_id={"dom": lax.rem(dom + OFFSETS[block] + DOM, DOM), "spec": spec},
            device_id_type=MESH,
        )

    def make_ghosts(step):
        pieces = join(dot(parts[:, :OWN], send_hot[...]))
        for row in range(BLOCKS):
            ghost_out[step, row] = pieces[:, row * SLOT : (row + 1) * SLOT]

    def send_ghosts(step):
        for row in range(BLOCKS):
            ghost_copy(step, row).start()

    def edge_weights(chunk, carry):
        parity = lax.rem(spec, 2) == 0
        east = jnp.where(parity, table[0], table[2])
        north = jnp.where(parity, table[1], table[3])
        at = lanes(chunk, 128)
        k = [
            east * normals[corner, 0:1, at] + north * normals[corner, 1:2, at]
            for corner in range(3)
        ]
        into = [jnp.maximum(value, 0.0) for value in k]
        away = [jnp.maximum(-value, 0.0) for value in k]
        for edge in range(3):
            a, b = edge, (edge + 1) % 3
            edge_weight[edge, :, at] = jnp.minimum(into[a], away[b]) - jnp.minimum(into[b], away[a])
        return carry

    def build_hot(chunk, carry):
        hot = []
        for corner in range(3):
            value = hot_rows(EXT, conn[corner : corner + 1, lanes(chunk, CHUNK)])
            corner_hot[:, lanes(chunk * 3 + corner, CHUNK)] = value
            hot.append(value)
        edge_hot[:, lanes(chunk * 2, CHUNK)] = hot[0] - hot[1]
        edge_hot[:, lanes(chunk * 2 + 1, CHUNK)] = hot[1] - hot[2]
        return carry

    def own_sweep(chunk, carry):
        at = lanes(chunk, 1024)
        own_diff[:, at] = join(dot(parts[:, :OWN], edge_hot[:OWN, at]))
        return carry

    def ghost_dot(chunk, target):
        target[...] = dot(parts[:, OWN:], edge_hot[OWN:, lanes(chunk, 2 * CHUNK)])

    def fluxes(chunk, ghost_diff):
        at = lanes(chunk, CHUNK)

        def corners(rows, high_rows, low_rows):
            size = rows.stop - rows.start
            first = rows.start % (2 * NDIR)
            d01, d12 = [
                own_diff[rows, lanes(2 * chunk + edge, CHUNK)]
                + (
                    ghost_diff[high_rows, edge * CHUNK : (edge + 1) * CHUNK]
                    + ghost_diff[low_rows, edge * CHUNK : (edge + 1) * CHUNK]
                )
                for edge in range(2)
            ]
            d20 = -(d01 + d12)
            w01, w12, w20 = [edge_weight[edge, first : first + size, at] for edge in range(3)]
            return [
                jnp.maximum(w01, 0.0) * d01 + jnp.minimum(w20, 0.0) * d20,
                jnp.maximum(w12, 0.0) * d12 + jnp.minimum(w01, 0.0) * d01,
                jnp.maximum(w20, 0.0) * d20 + jnp.minimum(w12, 0.0) * d12,
            ]

        for first in range(0, MAIN, 16):
            rows, low_rows = slice(first, first + 16), slice(MAIN + first, MAIN + first + 16)
            for corner, value in enumerate(corners(rows, rows, low_rows)):
                high = value.astype(bf16)
                column = lanes(chunk * 3 + corner, CHUNK)
                flux[rows, column] = high
                flux[low_rows, column] = (value - high.astype(f32)).astype(bf16)
        rows = slice(MAIN, PAD)
        high_rows, low_rows = slice(2 * MAIN, MAIN + PAD), slice(MAIN + PAD, BOTH)
        for corner, value in enumerate(corners(rows, high_rows, low_rows)):
            high = value.astype(bf16).astype(f32)
            column = lanes(chunk * 3 + corner, CHUNK)
            flux[2 * MAIN :, column] = jnp.concatenate([high, value - high], axis=0).astype(bf16)

    def sweep(pair, carry):
        ghost_dot(2 * pair + 1, odd_diff)
        fluxes(2 * pair, even_diff)
        ghost_dot(2 * pair + 2, even_diff)
        fluxes(2 * pair + 1, odd_diff)
        return carry

    first_bin = spec * ROWS
    first_freq = first_bin // NDIR
    row = lax.broadcasted_iota(jnp.int32, (PAD, 128), 0) + (first_bin - first_freq * NDIR)
    speed = jnp.full((PAD, 128), group_speed[first_freq], f32)
    for later in range(1, 6):
        value = group_speed[jnp.minimum(first_freq + later, NFREQ - 1)]
        speed = jnp.where(row >= later * NDIR, value, speed)

    make_ghosts(0)
    lax.fori_loop(0, CHUNKS, build_hot, 0)
    lax.fori_loop(0, ELEM // 128, edge_weights, 0)
    pl.semaphore_wait(barrier, BLOCKS + SPEC - 1)
    send_ghosts(0)

    for step in range(STEPS):
        lax.fori_loop(0, ELEM // 512, own_sweep, 0)
        for block in range(BLOCKS):
            ghost_copy(step, BLOCKS - 1 - block).wait_recv()
            parts[:, OWN + block * SLOT : OWN + (block + 1) * SLOT] = split(ghost_in[step, block])
        ghost_dot(0, even_diff)
        lax.fori_loop(0, CHUNKS // 2 - 1, sweep, 0)
        ghost_dot(CHUNKS - 1, odd_diff)
        fluxes(CHUNKS - 2, even_diff)
        fluxes(CHUNKS - 1, odd_diff)
        ghost_sum = join(dot_t(flux[...], corner_hot[OWN:, :]))
        for block in range(BLOCKS):
            back_out[step, block] = ghost_sum[:, block * SLOT : (block + 1) * SLOT]
            back_copy(step, block).start()

        def own_part(half, carry):
            rows = lanes(half, 512)
            own_sum[:, rows] = join(dot_t(flux[...], corner_hot[rows, :]))
            return carry

        lax.fori_loop(0, 2, own_part, 0)
        for block in range(BLOCKS):
            back_copy(step, block).wait_recv()
        returned = [split(back_in[step, row]) for row in range(BLOCKS)]
        returned = jnp.concatenate(returned, axis=1)
        for half in range(2):
            at = slice(half * 512, (half + 1) * 512)
            total = own_sum[:, at] + join(dot_t(returned, send_hot[at, :]))
            for quarter in range(4):
                chunk = half * 4 + quarter
                weight = step_weight[:, chunk * 128 : (chunk + 1) * 128]
                value = energy[chunk] - (speed * weight) * total[:, quarter * 128 : (quarter + 1) * 128]
                energy[chunk] = value
                if step + 1 < STEPS:
                    parts[:, chunk * 128 : (chunk + 1) * 128] = split(value)
        if step + 1 < STEPS:
            make_ghosts(step + 1)
            send_ghosts(step + 1)

    def spec_copy(shift):
        to = lax.rem(spec + shift, SPEC)
        return pltpu.make_async_remote_copy(
            src_ref=energy.at[to],
            dst_ref=landing.at[spec],
            send_sem=spec_send.at[shift - 1],
            recv_sem=spec_recv.at[shift - 1],
            device_id={"dom": dom, "spec": to},
            device_id_type=MESH,
        )

    for shift in (4, 3, 5, 2, 6, 1, 7):
        spec_copy(shift).start()
    landing[spec] = energy[spec]

    def partner_code(partner, first, sign):
        bin_ = lax.broadcasted_iota(jnp.int32, (1, 128), 1).astype(f32) + first
        freq = jnp.floor((bin_ + 0.5) * (1.0 / NDIR))
        partner = partner.astype(f32)
        other = jnp.floor((partner + 0.5) * (1.0 / NDIR))
        turn = sign * ((partner - NDIR * other) - (bin_ - NDIR * freq))
        turn = jnp.where(turn < 0, turn + NDIR, turn)
        return 4 * jnp.maximum(sign * (other - freq), 1.0) + turn

    def to_column(value, rule):
        for first in range(0, BINS, 128):
            start = min(first, BINS - 128)
            piece = rule(value[start : start + 128].reshape(1, 128), float(start))
            linear[start : start + 128] = jnp.broadcast_to(piece, (128, 128)).T

    def to_padded(target):
        def one(f, carry):
            base = pl.multiple_of((f + 2) * STRIDE, 8)
            value = linear[pl.ds(f * NDIR, NDIR)]
            target[pl.ds(base + LEAD, NDIR)] = value
            target[pl.ds(base + LEAD - 3, 3)] = value[NDIR - 3 :]
            target[pl.ds(base + LEAD + NDIR, 3)] = value[:3]
            return carry

        lax.fori_loop(0, NFREQ, one, 0)

    for target, value, rule in (
        (code_plus, dia_plus, functools.partial(partner_code, sign=1.0)),
        (code_minus, dia_minus, functools.partial(partner_code, sign=-1.0)),
        (coeff, dia_coeff, lambda value, first: value),
    ):
        target[...] = jnp.zeros((PADDED, 128), f32)
        to_column(value, rule)
        to_padded(target)

    for shift in range(1, SPEC):
        source = lax.rem(spec + SPEC - shift, SPEC)
        pltpu.make_async_remote_copy(
            src_ref=landing.at[source],
            dst_ref=landing.at[source],
            send_sem=spec_send.at[shift - 1],
            recv_sem=spec_recv.at[shift - 1],
            device_id={"dom": dom, "spec": source},
            device_id_type=MESH,
        ).wait_recv()

    half = NDIR // 2
    for source in range(SPEC):
        for piece in range(ROWS // half):
            f, second = divmod(source * (ROWS // half) + piece, 2)
            base = (f + 2) * STRIDE + LEAD
            value = landing[source, piece * half : (piece + 1) * half]
            padded[base + second * half : base + (second + 1) * half] = value
            if second:
                padded[base - 3 : base] = value[half - 3 :]
            else:
                padded[base + NDIR : base + NDIR + 3] = value[:3]
    for block in range(2):
        padded[block * STRIDE : (block + 1) * STRIDE] = padded[2 * STRIDE : 3 * STRIDE]
        last = (NFREQ + 2 + block) * STRIDE
        padded[last : last + STRIDE] = padded[(NFREQ + 1) * STRIDE : (NFREQ + 2) * STRIDE]

    wide = 40
    shifts = [(by, turn) for by in (1, 2) for turn in (1, 2, 3)]

    def terms(f, carry):
        base = pl.multiple_of((f + 2) * STRIDE + LEAD, 8)
        here = padded[pl.ds(base, wide)]
        plus = code_plus[pl.ds(base, wide)]
        minus = code_minus[pl.ds(base, wide)]
        upper = padded[pl.ds(base + STRIDE + 1, wide)]
        lower = padded[pl.ds(base - STRIDE - 1, wide)]
        for by, turn in shifts[1:]:
            code = float(4 * by + turn)
            upper = jnp.where(plus == code, padded[pl.ds(base + by * STRIDE + turn, wide)], upper)
            lower = jnp.where(minus == code, padded[pl.ds(base - by * STRIDE - turn, wide)], lower)
        value = coeff[pl.ds(base, wide)] * (
            here * here * (weight_plus * upper + weight_minus * lower)
            - 2.0 * weight_both * here * upper * lower
        )
        term[pl.ds(base, NDIR)] = value[:NDIR]
        term[pl.ds(base - 3, 3)] = value[NDIR - 3 : NDIR]
        term[pl.ds(base + NDIR, 3)] = value[:3]
        return carry

    lax.fori_loop(0, NFREQ, terms, 0)

    def gained(codes, at, code):
        rows = pl.ds(at, wide)
        return jnp.where(codes[rows] == code, term[rows], 0.0)

    def changes(f, carry):
        base = pl.multiple_of((f + 2) * STRIDE + LEAD, 8)
        value = padded[pl.ds(base, wide)] - 2.0 * term[pl.ds(base, wide)]
        for by, turn in shifts:
            code = float(4 * by + turn)
            value = value + gained(code_plus, base - by * STRIDE - turn, code)
            value = value + gained(code_minus, base + by * STRIDE + turn, code)
        out[pl.ds(f * NDIR, NDIR)] = value[:NDIR]
        return carry

    lax.fori_loop(0, NFREQ, changes, 0)
    high = (NFREQ + 1) * STRIDE + LEAD
    low = 2 * STRIDE + LEAD
    for turn in (1, 2, 3):
        code = float(4 + turn)
        out[BINS - NDIR :] = out[BINS - NDIR :] + gained(code_plus, high - turn, code)[:NDIR]
        out[:NDIR] = out[:NDIR] + gained(code_minus, low + turn, code)[:NDIR]

    for step in range(STEPS):
        for row in range(BLOCKS):
            ghost_copy(step, row).wait_send()
            back_copy(step, row).wait_send()
    for shift in range(1, SPEC):
        spec_copy(shift).wait_send()


def direction_table():
    rows = np.arange(TROWS)
    values = []
    for start in (0, NDIR // 2):
        angle = ((rows + start) % NDIR) * (2.0 * math.pi / NDIR)
        values += [np.cos(angle), np.sin(angle)]
    return np.repeat(np.stack(values)[:, :, None], 128, axis=2).astype(np.float32)


def on_device(
    spectrum, normals, conn, send_nodes, step_weight, group_speed, dia_plus, dia_minus, dia_coeff
):
    vmem = pl.BlockSpec(memory_space=pltpu.VMEM)
    smem = pl.BlockSpec(memory_space=pltpu.SMEM)
    return pl.pallas_call(
        kernel,
        out_shape=jax.ShapeDtypeStruct((BINS, SLOT), f32),
        in_specs=[vmem, vmem, vmem, vmem, vmem, smem, vmem, vmem, vmem, vmem],
        out_specs=vmem,
        scratch_shapes=[
            pltpu.VMEM((SPEC, PAD, 128), f32),
            pltpu.VMEM((BOTH, EXT), bf16),
            pltpu.VMEM((OWN, BLOCKS * SLOT), bf16),
            pltpu.VMEM((EXT, 3 * ELEM), bf16),
            pltpu.VMEM((EXT, 2 * ELEM), bf16),
            pltpu.VMEM((3, TROWS, ELEM), f32),
            pltpu.VMEM((PAD, 2 * ELEM), f32),
            pltpu.VMEM((BOTH, 2 * CHUNK), f32),
            pltpu.VMEM((BOTH, 2 * CHUNK), f32),
            pltpu.VMEM((BOTH, 3 * ELEM), bf16),
            pltpu.VMEM((PAD, OWN), f32),
            pltpu.VMEM((STEPS, BLOCKS, PAD, SLOT), f32),
            pltpu.VMEM((STEPS, BLOCKS, PAD, SLOT), f32),
            pltpu.VMEM((STEPS, BLOCKS, PAD, SLOT), f32),
            pltpu.VMEM((STEPS, BLOCKS, PAD, SLOT), f32),
            pltpu.VMEM((SPEC, PAD, 128), f32),
            pltpu.VMEM((BINS + 8, 128), f32),
            pltpu.VMEM((PADDED, 128), f32),
            pltpu.VMEM((PADDED, 128), f32),
            pltpu.VMEM((PADDED, 128), f32),
            pltpu.VMEM((PADDED, 128), f32),
            pltpu.VMEM((PADDED, 128), f32),
            pltpu.SemaphoreType.DMA((STEPS, 2, BLOCKS)),
            pltpu.SemaphoreType.DMA((STEPS, 2, BLOCKS)),
            pltpu.SemaphoreType.DMA((SPEC - 1,)),
            pltpu.SemaphoreType.DMA((SPEC - 1,)),
        ],
        compiler_params=pltpu.CompilerParams(
            collective_id=0, has_side_effects=True, vmem_limit_bytes=62 * 2**20
        ),
    )(
        spectrum,
        jnp.transpose(normals, (1, 0, 2)),
        conn,
        send_nodes,
        step_weight[None, :],
        group_speed,
        dia_plus,
        dia_minus,
        dia_coeff,
        jnp.asarray(direction_table()),
    )


def solution(mesh):
    in_specs = (
        P("spec", "dom"),
        P(None, None, "dom"),
        P(None, "dom"),
        P("dom", None, None),
        P("dom"),
        P(),
        P(),
        P(),
        P(),
    )
    out_specs = P(None, ("dom", "spec"))
    return jax.shard_map(
        on_device, mesh=mesh, in_specs=in_specs, out_specs=out_specs, check_vma=False
    )
```

```python
import functools
import math

import jax
import jax.numpy as jnp
import numpy as np
from jax import lax
from jax.experimental import pallas as pl
from jax.experimental.pallas import tpu as pltpu
from jax.sharding import PartitionSpec as P

NDIR = 36
NFREQ = 36
BINS = NDIR * NFREQ
STEPS = 2
DOM = 32
SPEC = 8
ROWS = BINS // SPEC
GROUPS = 2
MAIN = 80
TAIL = ROWS - 2 * MAIN
PAD = MAIN + 8
PARTS = 256
STEP8 = 16.0
OWN = 1024
SLOT = 128
BLOCKS = 4
EXT = OWN + BLOCKS * SLOT
ELEM = 2048
CHUNK = 256
CHUNKS = ELEM // CHUNK
TROWS = 88
OFFSETS = (-2, -1, 1, 2)
VALUE_LIMIT = 128.0
FLUX_SCALE = 0.25
STRIDE = 48
LEAD = 8
PADDED = (NFREQ + 4) * STRIDE + 8

weight_plus = 1.25 ** (-4)
weight_minus = 0.75 ** (-4)
weight_both = 0.9375 ** (-4)

MESH = pl.DeviceIdType.MESH
f32, bf16, f8 = jnp.float32, jnp.bfloat16, jnp.float8_e4m3fn


def split_two(value):
    high = value.astype(bf16).astype(f32)
    return jnp.concatenate([high, value - high], axis=0).astype(bf16)


def join_two(value):
    return value[:PAD] + value[PAD:]


def three(value):
    second = (value - value.astype(f8).astype(f32)) * STEP8
    third = (second - second.astype(f8).astype(f32)) * STEP8
    return value, second, third


def first_rows(value):
    return jnp.where(lax.broadcasted_iota(jnp.int32, value.shape, 0) < TAIL, value, 0.0)


def tail_parts(value):
    first, second, third = three(first_rows(value))
    return first + pltpu.roll(second, TAIL, 0) + pltpu.roll(third, 2 * TAIL, 0)


def join_tail(value):
    second, third = pltpu.roll(value, 8 - TAIL, 0), pltpu.roll(value, 8 - 2 * TAIL, 0)
    return first_rows(value + (second + third * (1 / STEP8)) * (1 / STEP8))


def split_three(value, group):
    zeros = jnp.zeros((8, value.shape[1]), f32)
    tail = tail_parts(value[MAIN:]) if group else zeros
    return jnp.concatenate([*three(value[:MAIN]), tail, zeros], axis=0).astype(f8)


def join_rows(value, first, size):
    at = [slice(part * MAIN + first, part * MAIN + first + size) for part in range(3)]
    return value[at[0]] + (value[at[1]] + value[at[2]] * (1 / STEP8)) * (1 / STEP8)


def join_three(value, group):
    zeros = jnp.zeros((8, value.shape[1]), f32)
    tail = join_tail(value[3 * MAIN : 3 * MAIN + 8]) if group else zeros
    return jnp.concatenate([join_rows(value, 0, MAIN), tail], axis=0)


def dot(left, right):
    return jnp.dot(left, right, preferred_element_type=f32)


def dot_t(left, right):
    return lax.dot_general(left, right, (((1,), (1,)), ((), ())), preferred_element_type=f32)


def lanes(index, size):
    return pl.ds(pl.multiple_of(index * size, size), size)


def kernel(
    spectrum,
    normals,
    conn,
    send_nodes,
    step_weight,
    group_speed,
    dia_plus,
    dia_minus,
    dia_coeff,
    table,
    out,
    energy,
    whole,
    parts,
    send_hot,
    corner_hot,
    edge_hot,
    edge_weight,
    even_diff,
    odd_diff,
    flux_parts,
    flux,
    own_sum,
    ghost_out,
    ghost_in,
    back_out,
    back_in,
    landing,
    linear,
    padded,
    term,
    code_plus,
    code_minus,
    coeff,
    halo_send,
    halo_recv,
    spec_send,
    spec_recv,
):
    dom = lax.axis_index("dom")
    spec = lax.axis_index("spec")

    barrier = pltpu.get_barrier_semaphore()
    for offset in OFFSETS:
        pl.semaphore_signal(
            barrier,
            inc=1,
            device_id={"dom": lax.rem(dom + offset + DOM, DOM), "spec": spec},
            device_id_type=MESH,
        )
    for shift in range(1, SPEC):
        pl.semaphore_signal(
            barrier,
            inc=1,
            device_id={"dom": dom, "spec": lax.rem(spec + shift, SPEC)},
            device_id_type=MESH,
        )

    for chunk in range(SPEC):
        at = slice(chunk * 128, (chunk + 1) * 128)
        energy[0, chunk, :MAIN] = spectrum[:MAIN, at]
        energy[0, chunk, MAIN:] = jnp.zeros((8, 128), f32)
        energy[1, chunk, : MAIN + TAIL] = spectrum[MAIN:, at]
        energy[1, chunk, MAIN + TAIL :] = jnp.zeros((8 - TAIL, 128), f32)
    flux_parts[3 * MAIN + 8 :] = jnp.zeros((PARTS - 3 * MAIN - 8, 3 * CHUNK), f32)

    for row in range(BLOCKS):
        index = jnp.broadcast_to(send_nodes[0, row : row + 1, :].astype(jnp.int16), (OWN, SLOT))
        node = lax.broadcasted_iota(jnp.int16, index.shape, 0)
        hot = jnp.where(node == index, bf16(1), bf16(0))
        send_hot[:, row * SLOT : (row + 1) * SLOT] = hot

    def halo_copy(group, step, back, block, source, target):
        return pltpu.make_async_remote_copy(
            src_ref=source.at[group, step, block],
            dst_ref=target.at[group, step, BLOCKS - 1 - block],
            send_sem=halo_send.at[group, step, back, block],
            recv_sem=halo_recv.at[group, step, back, block],
            device_id={"dom": lax.rem(dom + OFFSETS[block] + DOM, DOM), "spec": spec},
            device_id_type=MESH,
        )

    def ghost_copy(group, step, row):
        return halo_copy(group, step, 0, row, ghost_out, ghost_in)

    def back_copy(group, step, block):
        return halo_copy(group, step, 1, block, back_out, back_in)

    def make_ghosts(group, step):
        for chunk in range(SPEC):
            whole[:, chunk * 128 : (chunk + 1) * 128] = split_two(energy[group, chunk])
        pieces = join_two(dot(whole[...], send_hot[...]))
        for row in range(BLOCKS):
            ghost_out[group, step, row] = pieces[:, row * SLOT : (row + 1) * SLOT]

    def send_ghosts(group, step):
        for row in range(BLOCKS):
            ghost_copy(group, step, row).start()

    def edge_weights(chunk, carry):
        parity = lax.rem(spec, 2) == 0
        east = jnp.where(parity, table[0], table[2])
        north = jnp.where(parity, table[1], table[3])
        at = lanes(chunk, 128)
        k = [
            east * normals[corner, 0:1, at] + north * normals[corner, 1:2, at]
            for corner in range(3)
        ]
        into = [jnp.maximum(value, 0.0) for value in k]
        away = [jnp.maximum(-value, 0.0) for value in k]
        for edge in range(3):
            a, b = edge, (edge + 1) % 3
            value = jnp.minimum(into[a], away[b]) - jnp.minimum(into[b], away[a])
            edge_weight[edge, :, at] = FLUX_SCALE * value
        return carry

    def build_hot(chunk, carry):
        one, minus, zero = [jnp.full((128, CHUNK), value, f32).astype(f8) for value in (1, -1, 0)]
        node = lax.broadcasted_iota(jnp.int8, (128, CHUNK), 0)
        corners = [conn[corner : corner + 1, lanes(chunk, CHUNK)] for corner in range(3)]
        for first in range(0, EXT, 128):
            rows = slice(first, first + 128)
            hits = []
            for corner in range(3):
                local = corners[corner] - first
                local = jnp.where((local >= 0) & (local < 128), local, -1).astype(jnp.int8)
                hits.append(node == jnp.broadcast_to(local, (128, CHUNK)))
            for corner in range(3):
                value = jnp.where(hits[corner], one, zero)
                corner_hot[rows, lanes(chunk * 3 + corner, CHUNK)] = value
            for edge in range(2):
                a, b = hits[edge], hits[edge + 1]
                value = jnp.where(a, jnp.where(b, zero, one), jnp.where(b, minus, zero))
                edge_hot[rows, lanes(chunk * 2 + edge, CHUNK)] = value
        return carry

    def edge_dot(group, chunk, target):
        target[...] = dot(parts[group], edge_hot[:, lanes(chunk, 2 * CHUNK)])

    def fluxes(group, chunk, diff):
        at = lanes(chunk, CHUNK)

        def corners(first, size, d01, d12):
            start = (group * MAIN + first) % (2 * NDIR)
            d20 = -(d01 + d12)
            w01, w12, w20 = [edge_weight[edge, start : start + size, at] for edge in range(3)]
            return [
                jnp.maximum(w01, 0.0) * d01 + jnp.minimum(w20, 0.0) * d20,
                jnp.maximum(w12, 0.0) * d12 + jnp.minimum(w01, 0.0) * d01,
                jnp.maximum(w20, 0.0) * d20 + jnp.minimum(w12, 0.0) * d12,
            ]

        for first in range(0, MAIN, 16):
            edges = [
                join_rows(diff.at[:, edge * CHUNK : (edge + 1) * CHUNK], first, 16)
                for edge in range(2)
            ]
            for corner, value in enumerate(corners(first, 16, *edges)):
                column = slice(corner * CHUNK, (corner + 1) * CHUNK)
                for part, piece in enumerate(three(value)):
                    flux_parts[part * MAIN + first : part * MAIN + first + 16, column] = piece
        tail = slice(3 * MAIN, 3 * MAIN + 8)
        if group:
            edges = [
                join_tail(diff[tail, edge * CHUNK : (edge + 1) * CHUNK]) for edge in range(2)
            ]
            for corner, value in enumerate(corners(MAIN, 8, *edges)):
                flux_parts[tail, corner * CHUNK : (corner + 1) * CHUNK] = tail_parts(value)
        else:
            flux_parts[tail] = jnp.zeros((8, 3 * CHUNK), f32)
        flux[group, :, lanes(chunk, 3 * CHUNK)] = flux_parts[...].astype(f8)

    def gather(group):
        def pair(index, carry):
            edge_dot(group, 2 * index + 1, odd_diff)
            fluxes(group, 2 * index, even_diff)
            edge_dot(group, 2 * index + 2, even_diff)
            fluxes(group, 2 * index + 1, odd_diff)
            return carry

        edge_dot(group, 0, even_diff)
        lax.fori_loop(0, CHUNKS // 2 - 1, pair, 0)
        edge_dot(group, CHUNKS - 1, odd_diff)
        fluxes(group, CHUNKS - 2, even_diff)
        fluxes(group, CHUNKS - 1, odd_diff)

    first_bin = spec * ROWS
    first_freq = first_bin // NDIR
    speeds = []
    for group in range(GROUPS):
        start = first_bin - first_freq * NDIR + group * MAIN
        row = lax.broadcasted_iota(jnp.int32, (PAD, 128), 0) + start
        speed = jnp.full((PAD, 128), group_speed[first_freq], f32)
        for later in range(1, 6):
            value = group_speed[jnp.minimum(first_freq + later, NFREQ - 1)]
            speed = jnp.where(row >= later * NDIR, value, speed)
        speeds.append(speed)

    unscale = [None] * GROUPS

    def ready(group, step):
        for row in range(BLOCKS):
            ghost_copy(group, step, row).wait_recv()
        chunks = [energy.at[group, chunk] for chunk in range(SPEC)]
        chunks += [ghost_in.at[group, step, block] for block in range(BLOCKS)]
        largest = jnp.abs(chunks[0][...])
        for ref in chunks[1:]:
            largest = jnp.maximum(largest, jnp.abs(ref[...]))
        largest = jnp.maximum(jnp.max(largest, axis=(0, 1), keepdims=True), 1e-30)
        scale = VALUE_LIMIT / largest
        unscale[group] = largest * (1 / (VALUE_LIMIT * FLUX_SCALE))
        for chunk, ref in enumerate(chunks):
            parts[group, :, chunk * 128 : (chunk + 1) * 128] = split_three(ref[...] * scale, group)

    def ghost_scatter(group, step):
        total = dot_t(flux[group], corner_hot[OWN:, :])
        total = join_three(total, group) * unscale[group]
        for block in range(BLOCKS):
            back_out[group, step, block] = total[:, block * SLOT : (block + 1) * SLOT]
            back_copy(group, step, block).start()

    def own_scatter(group):
        def half(index, carry):
            rows = lanes(index, 512)
            own_sum[group, :, rows] = join_three(dot_t(flux[group], corner_hot[rows, :]), group)
            return carry

        lax.fori_loop(0, 2, half, 0)

    def update(group, step):
        for block in range(BLOCKS):
            back_copy(group, step, block).wait_recv()
        returned = [split_two(back_in[group, step, row]) for row in range(BLOCKS)]
        returned = jnp.concatenate(returned, axis=1)
        for half in range(2):
            at = slice(half * 512, (half + 1) * 512)
            total = own_sum[group, :, at] * unscale[group]
            total = total + join_two(dot_t(returned, send_hot[at, :]))
            for quarter in range(4):
                chunk = half * 4 + quarter
                weight = speeds[group] * step_weight[:, chunk * 128 : (chunk + 1) * 128]
                change = weight * total[:, quarter * 128 : (quarter + 1) * 128]
                energy[group, chunk] = energy[group, chunk] - change

    def spec_copy(group, shift):
        to = lax.rem(spec + shift, SPEC)
        count = MAIN + 8 * group
        return pltpu.make_async_remote_copy(
            src_ref=energy.at[group, to, pl.ds(0, count)],
            dst_ref=landing.at[spec, pl.ds(group * MAIN, count)],
            send_sem=spec_send.at[group, shift - 1],
            recv_sem=spec_recv.at[group, shift - 1],
            device_id={"dom": dom, "spec": to},
            device_id_type=MESH,
        )

    def spread(group):
        for shift in (4, 3, 5, 2, 6, 1, 7):
            spec_copy(group, shift).start()
        count = MAIN + 8 * group
        landing[spec, pl.ds(group * MAIN, count)] = energy[group, spec, :count]

    for group in range(GROUPS):
        make_ghosts(group, 0)
    lax.fori_loop(0, CHUNKS, build_hot, 0)
    lax.fori_loop(0, ELEM // 128, edge_weights, 0)
    pl.semaphore_wait(barrier, BLOCKS + SPEC - 1)
    for group in range(GROUPS):
        send_ghosts(group, 0)

    for step in range(STEPS):
        for group in range(GROUPS):
            ready(group, step)
            gather(group)
            ghost_scatter(group, step)
        for group in range(GROUPS):
            own_scatter(group)
            update(group, step)
            if step + 1 < STEPS:
                make_ghosts(group, step + 1)
                send_ghosts(group, step + 1)
            else:
                spread(group)

    def partner_code(partner, first, sign):
        bin_ = lax.broadcasted_iota(jnp.int32, (1, 128), 1).astype(f32) + first
        freq = jnp.floor((bin_ + 0.5) * (1.0 / NDIR))
        partner = partner.astype(f32)
        other = jnp.floor((partner + 0.5) * (1.0 / NDIR))
        turn = sign * ((partner - NDIR * other) - (bin_ - NDIR * freq))
        turn = jnp.where(turn < 0, turn + NDIR, turn)
        return 4 * jnp.maximum(sign * (other - freq), 1.0) + turn

    def to_column(value, rule):
        for first in range(0, BINS, 128):
            start = min(first, BINS - 128)
            piece = rule(value[start : start + 128].reshape(1, 128), float(start))
            linear[start : start + 128] = jnp.broadcast_to(piece, (128, 128)).T

    def to_padded(target):
        def one(f, carry):
            base = pl.multiple_of((f + 2) * STRIDE, 8)
            value = linear[pl.ds(f * NDIR, NDIR)]
            target[pl.ds(base + LEAD, NDIR)] = value
            target[pl.ds(base + LEAD - 3, 3)] = value[NDIR - 3 :]
            target[pl.ds(base + LEAD + NDIR, 3)] = value[:3]
            return carry

        lax.fori_loop(0, NFREQ, one, 0)

    for target, value, rule in (
        (code_plus, dia_plus, functools.partial(partner_code, sign=1.0)),
        (code_minus, dia_minus, functools.partial(partner_code, sign=-1.0)),
        (coeff, dia_coeff, lambda value, first: value),
    ):
        target[...] = jnp.zeros((PADDED, 128), f32)
        to_column(value, rule)
        to_padded(target)

    for group in range(GROUPS):
        for shift in range(1, SPEC):
            source = lax.rem(spec + SPEC - shift, SPEC)
            place = landing.at[source, pl.ds(group * MAIN, MAIN + 8 * group)]
            pltpu.make_async_remote_copy(
                src_ref=place,
                dst_ref=place,
                send_sem=spec_send.at[group, shift - 1],
                recv_sem=spec_recv.at[group, shift - 1],
                device_id={"dom": dom, "spec": source},
                device_id_type=MESH,
            ).wait_recv()

    half = NDIR // 2
    for source in range(SPEC):
        for piece in range(ROWS // half):
            f, second = divmod(source * (ROWS // half) + piece, 2)
            base = (f + 2) * STRIDE + LEAD
            value = landing[source, piece * half : (piece + 1) * half]
            padded[base + second * half : base + (second + 1) * half] = value
            if second:
                padded[base - 3 : base] = value[half - 3 :]
            else:
                padded[base + NDIR : base + NDIR + 3] = value[:3]
    for block in range(2):
        padded[block * STRIDE : (block + 1) * STRIDE] = padded[2 * STRIDE : 3 * STRIDE]
        last = (NFREQ + 2 + block) * STRIDE
        padded[last : last + STRIDE] = padded[(NFREQ + 1) * STRIDE : (NFREQ + 2) * STRIDE]

    wide = 40
    shifts = [(by, turn) for by in (1, 2) for turn in (1, 2, 3)]

    def terms(f, carry):
        base = pl.multiple_of((f + 2) * STRIDE + LEAD, 8)
        here = padded[pl.ds(base, wide)]
        plus = code_plus[pl.ds(base, wide)]
        minus = code_minus[pl.ds(base, wide)]
        upper = padded[pl.ds(base + STRIDE + 1, wide)]
        lower = padded[pl.ds(base - STRIDE - 1, wide)]
        for by, turn in shifts[1:]:
            code = float(4 * by + turn)
            upper = jnp.where(plus == code, padded[pl.ds(base + by * STRIDE + turn, wide)], upper)
            lower = jnp.where(minus == code, padded[pl.ds(base - by * STRIDE - turn, wide)], lower)
        value = coeff[pl.ds(base, wide)] * (
            here * here * (weight_plus * upper + weight_minus * lower)
            - 2.0 * weight_both * here * upper * lower
        )
        term[pl.ds(base, NDIR)] = value[:NDIR]
        term[pl.ds(base - 3, 3)] = value[NDIR - 3 : NDIR]
        term[pl.ds(base + NDIR, 3)] = value[:3]
        return carry

    lax.fori_loop(0, NFREQ, terms, 0)

    def gained(codes, at, code):
        rows = pl.ds(at, wide)
        return jnp.where(codes[rows] == code, term[rows], 0.0)

    def changes(f, carry):
        base = pl.multiple_of((f + 2) * STRIDE + LEAD, 8)
        value = padded[pl.ds(base, wide)] - 2.0 * term[pl.ds(base, wide)]
        for by, turn in shifts:
            code = float(4 * by + turn)
            value = value + gained(code_plus, base - by * STRIDE - turn, code)
            value = value + gained(code_minus, base + by * STRIDE + turn, code)
        out[pl.ds(f * NDIR, NDIR)] = value[:NDIR]
        return carry

    lax.fori_loop(0, NFREQ, changes, 0)
    high = (NFREQ + 1) * STRIDE + LEAD
    low = 2 * STRIDE + LEAD
    for turn in (1, 2, 3):
        code = float(4 + turn)
        out[BINS - NDIR :] = out[BINS - NDIR :] + gained(code_plus, high - turn, code)[:NDIR]
        out[:NDIR] = out[:NDIR] + gained(code_minus, low + turn, code)[:NDIR]

    for group in range(GROUPS):
        for step in range(STEPS):
            for row in range(BLOCKS):
                ghost_copy(group, step, row).wait_send()
                back_copy(group, step, row).wait_send()
        for shift in range(1, SPEC):
            spec_copy(group, shift).wait_send()


def direction_table():
    rows = np.arange(TROWS)
    values = []
    for start in (0, NDIR // 2):
        angle = ((rows + start) % NDIR) * (2.0 * math.pi / NDIR)
        values += [np.cos(angle), np.sin(angle)]
    return np.repeat(np.stack(values)[:, :, None], 128, axis=2).astype(np.float32)


def on_device(
    spectrum, normals, conn, send_nodes, step_weight, group_speed, dia_plus, dia_minus, dia_coeff
):
    vmem = pl.BlockSpec(memory_space=pltpu.VMEM)
    smem = pl.BlockSpec(memory_space=pltpu.SMEM)
    return pl.pallas_call(
        kernel,
        out_shape=jax.ShapeDtypeStruct((BINS, SLOT), f32),
        in_specs=[vmem, vmem, vmem, vmem, vmem, smem, vmem, vmem, vmem, vmem],
        out_specs=vmem,
        scratch_shapes=[
            pltpu.VMEM((GROUPS, SPEC, PAD, 128), f32),
            pltpu.VMEM((2 * PAD, OWN), bf16),
            pltpu.VMEM((GROUPS, PARTS, EXT), f8),
            pltpu.VMEM((OWN, BLOCKS * SLOT), bf16),
            pltpu.VMEM((EXT, 3 * ELEM), f8),
            pltpu.VMEM((EXT, 2 * ELEM), f8),
            pltpu.VMEM((3, TROWS, ELEM), f32),
            pltpu.VMEM((PARTS, 2 * CHUNK), f32),
            pltpu.VMEM((PARTS, 2 * CHUNK), f32),
            pltpu.VMEM((PARTS, 3 * CHUNK), f32),
            pltpu.VMEM((GROUPS, PARTS, 3 * ELEM), f8),
            pltpu.VMEM((GROUPS, PAD, OWN), f32),
            pltpu.VMEM((GROUPS, STEPS, BLOCKS, PAD, SLOT), f32),
            pltpu.VMEM((GROUPS, STEPS, BLOCKS, PAD, SLOT), f32),
            pltpu.VMEM((GROUPS, STEPS, BLOCKS, PAD, SLOT), f32),
            pltpu.VMEM((GROUPS, STEPS, BLOCKS, PAD, SLOT), f32),
            pltpu.VMEM((SPEC, ROWS + 6, 128), f32),
            pltpu.VMEM((BINS + 8, 128), f32),
            pltpu.VMEM((PADDED, 128), f32),
            pltpu.VMEM((PADDED, 128), f32),
            pltpu.VMEM((PADDED, 128), f32),
            pltpu.VMEM((PADDED, 128), f32),
            pltpu.VMEM((PADDED, 128), f32),
            pltpu.SemaphoreType.DMA((GROUPS, STEPS, 2, BLOCKS)),
            pltpu.SemaphoreType.DMA((GROUPS, STEPS, 2, BLOCKS)),
            pltpu.SemaphoreType.DMA((GROUPS, SPEC - 1)),
            pltpu.SemaphoreType.DMA((GROUPS, SPEC - 1)),
        ],
        compiler_params=pltpu.CompilerParams(
            collective_id=0, has_side_effects=True, vmem_limit_bytes=62 * 2**20
        ),
    )(
        spectrum,
        jnp.transpose(normals, (1, 0, 2)),
        conn,
        send_nodes,
        step_weight[None, :],
        group_speed,
        dia_plus,
        dia_minus,
        dia_coeff,
        jnp.asarray(direction_table()),
    )


def solution(mesh):
    in_specs = (
        P("spec", "dom"),
        P(None, None, "dom"),
        P(None, "dom"),
        P("dom", None, None),
        P("dom"),
        P(),
        P(),
        P(),
        P(),
    )
    out_specs = P(None, ("dom", "spec"))
    return jax.shard_map(
        on_device, mesh=mesh, in_specs=in_specs, out_specs=out_specs, check_vma=False
    )
```

```python
import functools
import math

import jax
import jax.numpy as jnp
import numpy as np
from jax import lax
from jax.experimental import pallas as pl
from jax.experimental.pallas import tpu as pltpu
from jax.sharding import PartitionSpec as P

NDIR = 36
NFREQ = 36
BINS = NDIR * NFREQ
STEPS = 2
DOM = 32
SPEC = 8
ROWS = BINS // SPEC
GROUPS = 2
MAIN = 80
TAIL = ROWS - 2 * MAIN
PAD = MAIN + 8
PARTS = 256
STEP8 = 16.0
OWN = 1024
SLOT = 128
BLOCKS = 4
EXT = OWN + BLOCKS * SLOT
ELEM = 2048
CHUNK = 256
CHUNKS = ELEM // CHUNK
TROWS = 88
OFFSETS = (-2, -1, 1, 2)
VALUE_LIMIT = 128.0
FLUX_LIMIT = 240.0
WHOLE = 1.5 * 2.0**23
STRIDE = 48
LEAD = 8
PADDED = (NFREQ + 4) * STRIDE + 8

weight_plus = 1.25 ** (-4)
weight_minus = 0.75 ** (-4)
weight_both = 0.9375 ** (-4)

MESH = pl.DeviceIdType.MESH
f32, bf16, f8 = jnp.float32, jnp.bfloat16, jnp.float8_e4m3fn


def split_two(value):
    high = value.astype(bf16).astype(f32)
    return jnp.concatenate([high, value - high], axis=0).astype(bf16)


def join_two(value):
    return value[:PAD] + value[PAD:]


def whole_number(value):
    return (value + WHOLE) - WHOLE


def three(value):
    first = whole_number(value)
    rest = (value - first.astype(f8).astype(f32)) * STEP8
    second = whole_number(rest)
    third = (rest - second.astype(f8).astype(f32)) * STEP8
    return first, second, third


def first_rows(value):
    return jnp.where(lax.broadcasted_iota(jnp.int32, value.shape, 0) < TAIL, value, 0.0)


def tail_parts(value):
    first, second, third = three(first_rows(value))
    return first + pltpu.roll(second, TAIL, 0) + pltpu.roll(third, 2 * TAIL, 0)


def join_tail(value):
    second, third = pltpu.roll(value, 8 - TAIL, 0), pltpu.roll(value, 8 - 2 * TAIL, 0)
    return first_rows(value + (second + third * (1 / STEP8)) * (1 / STEP8))


def split_three(value, group):
    zeros = jnp.zeros((8, value.shape[1]), f32)
    tail = tail_parts(value[MAIN:]) if group else zeros
    return jnp.concatenate([*three(value[:MAIN]), tail, zeros], axis=0).astype(f8)


def join_rows(value, first, size):
    at = [slice(part * MAIN + first, part * MAIN + first + size) for part in range(3)]
    return value[at[0]] + (value[at[1]] + value[at[2]] * (1 / STEP8)) * (1 / STEP8)


def join_three(value, group):
    zeros = jnp.zeros((8, value.shape[1]), f32)
    tail = join_tail(value[3 * MAIN : 3 * MAIN + 8]) if group else zeros
    return jnp.concatenate([join_rows(value, 0, MAIN), tail], axis=0)


def dot(left, right):
    return jnp.dot(left, right, preferred_element_type=f32)


def dot_t(left, right):
    return lax.dot_general(left, right, (((1,), (1,)), ((), ())), preferred_element_type=f32)


def lanes(index, size):
    return pl.ds(pl.multiple_of(index * size, size), size)


def kernel(
    spectrum,
    normals,
    conn,
    send_nodes,
    step_weight,
    group_speed,
    dia_plus,
    dia_minus,
    dia_coeff,
    table,
    out,
    energy,
    whole,
    parts,
    send_hot,
    corner_hot,
    edge_hot,
    edge_weight,
    even_diff,
    odd_diff,
    flux_parts,
    flux,
    own_sum,
    ghost_out,
    ghost_in,
    back_out,
    back_in,
    landing,
    linear,
    padded,
    term,
    code_plus,
    code_minus,
    coeff,
    halo_send,
    halo_recv,
    spec_send,
    spec_recv,
):
    dom = lax.axis_index("dom")
    spec = lax.axis_index("spec")

    barrier = pltpu.get_barrier_semaphore()
    for offset in OFFSETS:
        pl.semaphore_signal(
            barrier,
            inc=1,
            device_id={"dom": lax.rem(dom + offset + DOM, DOM), "spec": spec},
            device_id_type=MESH,
        )
    for shift in range(1, SPEC):
        pl.semaphore_signal(
            barrier,
            inc=1,
            device_id={"dom": dom, "spec": lax.rem(spec + shift, SPEC)},
            device_id_type=MESH,
        )

    for chunk in range(SPEC):
        at = slice(chunk * 128, (chunk + 1) * 128)
        energy[0, chunk, :MAIN] = spectrum[:MAIN, at]
        energy[0, chunk, MAIN:] = jnp.zeros((8, 128), f32)
        energy[1, chunk, : MAIN + TAIL] = spectrum[MAIN:, at]
        energy[1, chunk, MAIN + TAIL :] = jnp.zeros((8 - TAIL, 128), f32)
    flux_parts[3 * MAIN + 8 :] = jnp.zeros((PARTS - 3 * MAIN - 8, 3 * CHUNK), f32)

    for row in range(BLOCKS):
        index = jnp.broadcast_to(send_nodes[0, row : row + 1, :].astype(jnp.int16), (OWN, SLOT))
        node = lax.broadcasted_iota(jnp.int16, index.shape, 0)
        hot = jnp.where(node == index, bf16(1), bf16(0))
        send_hot[:, row * SLOT : (row + 1) * SLOT] = hot

    def halo_copy(group, step, back, block, source, target):
        return pltpu.make_async_remote_copy(
            src_ref=source.at[group, step, block],
            dst_ref=target.at[group, step, BLOCKS - 1 - block],
            send_sem=halo_send.at[group, step, back, block],
            recv_sem=halo_recv.at[group, step, back, block],
            device_id={"dom": lax.rem(dom + OFFSETS[block] + DOM, DOM), "spec": spec},
            device_id_type=MESH,
        )

    def ghost_copy(group, step, row):
        return halo_copy(group, step, 0, row, ghost_out, ghost_in)

    def back_copy(group, step, block):
        return halo_copy(group, step, 1, block, back_out, back_in)

    def make_ghosts(group, step):
        for chunk in range(SPEC):
            whole[:, chunk * 128 : (chunk + 1) * 128] = split_two(energy[group, chunk])
        pieces = join_two(dot(whole[...], send_hot[...]))
        for row in range(BLOCKS):
            ghost_out[group, step, row] = pieces[:, row * SLOT : (row + 1) * SLOT]

    def send_ghosts(group, step):
        for row in range(BLOCKS):
            ghost_copy(group, step, row).start()

    longest = normals[:, 0] * normals[:, 0] + normals[:, 1] * normals[:, 1]
    longest = jnp.sqrt(jnp.max(longest, axis=(0, 1), keepdims=True))
    flux_scale = (FLUX_LIMIT / (2 * VALUE_LIMIT)) / longest

    def edge_weights(chunk, carry):
        parity = lax.rem(spec, 2) == 0
        east = jnp.where(parity, table[0], table[2])
        north = jnp.where(parity, table[1], table[3])
        at = lanes(chunk, 128)
        k = [
            east * normals[corner, 0:1, at] + north * normals[corner, 1:2, at]
            for corner in range(3)
        ]
        into = [jnp.maximum(value, 0.0) for value in k]
        away = [jnp.maximum(-value, 0.0) for value in k]
        for edge in range(3):
            a, b = edge, (edge + 1) % 3
            value = jnp.minimum(into[a], away[b]) - jnp.minimum(into[b], away[a])
            edge_weight[edge, :, at] = flux_scale * value
        return carry

    def build_hot(chunk, carry):
        one, minus, zero = [jnp.full((128, CHUNK), value, f32).astype(f8) for value in (1, -1, 0)]
        node = lax.broadcasted_iota(jnp.int8, (128, CHUNK), 0)
        corners = [conn[corner : corner + 1, lanes(chunk, CHUNK)] for corner in range(3)]
        for first in range(0, EXT, 128):
            rows = slice(first, first + 128)
            hits = []
            for corner in range(3):
                local = corners[corner] - first
                local = jnp.where((local >= 0) & (local < 128), local, -1).astype(jnp.int8)
                hits.append(node == jnp.broadcast_to(local, (128, CHUNK)))
            for corner in range(3):
                value = jnp.where(hits[corner], one, zero)
                corner_hot[rows, lanes(chunk * 3 + corner, CHUNK)] = value
            for edge in range(2):
                a, b = hits[edge], hits[edge + 1]
                value = jnp.where(a, jnp.where(b, zero, one), jnp.where(b, minus, zero))
                edge_hot[rows, lanes(chunk * 2 + edge, CHUNK)] = value
        return carry

    def edge_dot(group, chunk, target):
        target[...] = dot(parts[group], edge_hot[:, lanes(chunk, 2 * CHUNK)])

    def fluxes(group, chunk, diff):
        at = lanes(chunk, CHUNK)

        def corners(first, size, d01, d12):
            start = (group * MAIN + first) % (2 * NDIR)
            d20 = -(d01 + d12)
            w01, w12, w20 = [edge_weight[edge, start : start + size, at] for edge in range(3)]
            return [
                jnp.maximum(w01, 0.0) * d01 + jnp.minimum(w20, 0.0) * d20,
                jnp.maximum(w12, 0.0) * d12 + jnp.minimum(w01, 0.0) * d01,
                jnp.maximum(w20, 0.0) * d20 + jnp.minimum(w12, 0.0) * d12,
            ]

        for first in range(0, MAIN, 16):
            edges = [
                join_rows(diff.at[:, edge * CHUNK : (edge + 1) * CHUNK], first, 16)
                for edge in range(2)
            ]
            for corner, value in enumerate(corners(first, 16, *edges)):
                column = slice(corner * CHUNK, (corner + 1) * CHUNK)
                for part, piece in enumerate(three(value)):
                    flux_parts[part * MAIN + first : part * MAIN + first + 16, column] = piece
        tail = slice(3 * MAIN, 3 * MAIN + 8)
        if group:
            edges = [
                join_tail(diff[tail, edge * CHUNK : (edge + 1) * CHUNK]) for edge in range(2)
            ]
            for corner, value in enumerate(corners(MAIN, 8, *edges)):
                flux_parts[tail, corner * CHUNK : (corner + 1) * CHUNK] = tail_parts(value)
        else:
            flux_parts[tail] = jnp.zeros((8, 3 * CHUNK), f32)
        flux[group, :, lanes(chunk, 3 * CHUNK)] = flux_parts[...].astype(f8)

    def gather(group):
        def pair(index, carry):
            edge_dot(group, 2 * index + 1, odd_diff)
            fluxes(group, 2 * index, even_diff)
            edge_dot(group, 2 * index + 2, even_diff)
            fluxes(group, 2 * index + 1, odd_diff)
            return carry

        edge_dot(group, 0, even_diff)
        lax.fori_loop(0, CHUNKS // 2 - 1, pair, 0)
        edge_dot(group, CHUNKS - 1, odd_diff)
        fluxes(group, CHUNKS - 2, even_diff)
        fluxes(group, CHUNKS - 1, odd_diff)

    first_bin = spec * ROWS
    first_freq = first_bin // NDIR
    speeds = []
    for group in range(GROUPS):
        start = first_bin - first_freq * NDIR + group * MAIN
        row = lax.broadcasted_iota(jnp.int32, (PAD, 128), 0) + start
        speed = jnp.full((PAD, 128), group_speed[first_freq], f32)
        for later in range(1, 6):
            value = group_speed[jnp.minimum(first_freq + later, NFREQ - 1)]
            speed = jnp.where(row >= later * NDIR, value, speed)
        speeds.append(speed)

    unscale = [None] * GROUPS

    def ready(group, step):
        for row in range(BLOCKS):
            ghost_copy(group, step, row).wait_recv()
        chunks = [energy.at[group, chunk] for chunk in range(SPEC)]
        chunks += [ghost_in.at[group, step, block] for block in range(BLOCKS)]
        most = least = chunks[0][:MAIN]
        for ref in chunks:
            most = jnp.maximum(most, ref[:MAIN])
            least = jnp.minimum(least, ref[:MAIN])
            if group:
                tail = ref[MAIN : MAIN + TAIL]
                most = jnp.maximum(most, jnp.max(tail, axis=0, keepdims=True))
                least = jnp.minimum(least, jnp.min(tail, axis=0, keepdims=True))
        most = jnp.max(most, axis=(0, 1), keepdims=True)
        least = jnp.min(least, axis=(0, 1), keepdims=True)
        middle = 0.5 * (most + least)
        reach = jnp.maximum(0.5001 * (most - least), 1e-30)
        scale = VALUE_LIMIT / reach
        unscale[group] = reach * longest * (2 / FLUX_LIMIT)
        for chunk, ref in enumerate(chunks):
            value = (ref[...] - middle) * scale
            parts[group, :, chunk * 128 : (chunk + 1) * 128] = split_three(value, group)

    def ghost_scatter(group, step):
        total = dot_t(flux[group], corner_hot[OWN:, :])
        total = join_three(total, group) * unscale[group]
        for block in range(BLOCKS):
            back_out[group, step, block] = total[:, block * SLOT : (block + 1) * SLOT]
            back_copy(group, step, block).start()

    def own_scatter(group):
        def half(index, carry):
            rows = lanes(index, 512)
            own_sum[group, :, rows] = join_three(dot_t(flux[group], corner_hot[rows, :]), group)
            return carry

        lax.fori_loop(0, 2, half, 0)

    def update(group, step):
        for block in range(BLOCKS):
            back_copy(group, step, block).wait_recv()
        returned = [split_two(back_in[group, step, row]) for row in range(BLOCKS)]
        returned = jnp.concatenate(returned, axis=1)
        for half in range(2):
            at = slice(half * 512, (half + 1) * 512)
            total = own_sum[group, :, at] * unscale[group]
            total = total + join_two(dot_t(returned, send_hot[at, :]))
            for quarter in range(4):
                chunk = half * 4 + quarter
                weight = speeds[group] * step_weight[:, chunk * 128 : (chunk + 1) * 128]
                change = weight * total[:, quarter * 128 : (quarter + 1) * 128]
                energy[group, chunk] = energy[group, chunk] - change

    def spec_copy(group, shift):
        to = lax.rem(spec + shift, SPEC)
        count = MAIN + TAIL * group
        return pltpu.make_async_remote_copy(
            src_ref=energy.at[group, to, pl.ds(0, count)],
            dst_ref=landing.at[spec, pl.ds(group * MAIN, count)],
            send_sem=spec_send.at[group, shift - 1],
            recv_sem=spec_recv.at[group, shift - 1],
            device_id={"dom": dom, "spec": to},
            device_id_type=MESH,
        )

    def spread(group):
        for shift in (4, 3, 5, 2, 6, 1, 7):
            spec_copy(group, shift).start()
        count = MAIN + TAIL * group
        landing[spec, pl.ds(group * MAIN, count)] = energy[group, spec, :count]

    for group in range(GROUPS):
        make_ghosts(group, 0)
    lax.fori_loop(0, CHUNKS, build_hot, 0)
    lax.fori_loop(0, ELEM // 128, edge_weights, 0)
    pl.semaphore_wait(barrier, BLOCKS + SPEC - 1)
    for group in range(GROUPS):
        send_ghosts(group, 0)

    for group in range(GROUPS):
        ready(group, 0)
        gather(group)
        ghost_scatter(group, 0)
    for group in range(GROUPS):
        own_scatter(group)
        update(group, 0)
        make_ghosts(group, 1)
        send_ghosts(group, 1)
    ready(0, 1)
    gather(0)
    ghost_scatter(0, 1)
    own_scatter(0)
    ready(1, 1)
    gather(1)
    update(0, 1)
    spread(0)
    ghost_scatter(1, 1)
    own_scatter(1)
    update(1, 1)
    spread(1)

    def partner_code(partner, first, sign):
        bin_ = lax.broadcasted_iota(jnp.int32, (1, 128), 1).astype(f32) + first
        freq = jnp.floor((bin_ + 0.5) * (1.0 / NDIR))
        partner = partner.astype(f32)
        other = jnp.floor((partner + 0.5) * (1.0 / NDIR))
        turn = sign * ((partner - NDIR * other) - (bin_ - NDIR * freq))
        turn = jnp.where(turn < 0, turn + NDIR, turn)
        return 4 * jnp.maximum(sign * (other - freq), 1.0) + turn

    def to_column(value, rule):
        for first in range(0, BINS, 128):
            start = min(first, BINS - 128)
            piece = rule(value[start : start + 128].reshape(1, 128), float(start))
            linear[start : start + 128] = jnp.broadcast_to(piece, (128, 128)).T

    def to_padded(target):
        def one(f, carry):
            base = pl.multiple_of((f + 2) * STRIDE, 8)
            value = linear[pl.ds(f * NDIR, NDIR)]
            target[pl.ds(base + LEAD, NDIR)] = value
            target[pl.ds(base + LEAD - 3, 3)] = value[NDIR - 3 :]
            target[pl.ds(base + LEAD + NDIR, 3)] = value[:3]
            return carry

        lax.fori_loop(0, NFREQ, one, 0)

    for target, value, rule in (
        (code_plus, dia_plus, functools.partial(partner_code, sign=1.0)),
        (code_minus, dia_minus, functools.partial(partner_code, sign=-1.0)),
        (coeff, dia_coeff, lambda value, first: value),
    ):
        target[...] = jnp.zeros((PADDED, 128), f32)
        to_column(value, rule)
        to_padded(target)

    for group in range(GROUPS):
        for shift in range(1, SPEC):
            source = lax.rem(spec + SPEC - shift, SPEC)
            place = landing.at[source, pl.ds(group * MAIN, MAIN + TAIL * group)]
            pltpu.make_async_remote_copy(
                src_ref=place,
                dst_ref=place,
                send_sem=spec_send.at[group, shift - 1],
                recv_sem=spec_recv.at[group, shift - 1],
                device_id={"dom": dom, "spec": source},
                device_id_type=MESH,
            ).wait_recv()

    half = NDIR // 2
    for source in range(SPEC):
        for piece in range(ROWS // half):
            f, second = divmod(source * (ROWS // half) + piece, 2)
            base = (f + 2) * STRIDE + LEAD
            value = landing[source, piece * half : (piece + 1) * half]
            padded[base + second * half : base + (second + 1) * half] = value
            if second:
                padded[base - 3 : base] = value[half - 3 :]
            else:
                padded[base + NDIR : base + NDIR + 3] = value[:3]
    for block in range(2):
        padded[block * STRIDE : (block + 1) * STRIDE] = padded[2 * STRIDE : 3 * STRIDE]
        last = (NFREQ + 2 + block) * STRIDE
        padded[last : last + STRIDE] = padded[(NFREQ + 1) * STRIDE : (NFREQ + 2) * STRIDE]

    wide = 40
    shifts = [(by, turn) for by in (1, 2) for turn in (1, 2, 3)]

    def terms(f, carry):
        base = pl.multiple_of((f + 2) * STRIDE + LEAD, 8)
        here = padded[pl.ds(base, wide)]
        plus = code_plus[pl.ds(base, wide)]
        minus = code_minus[pl.ds(base, wide)]
        upper = padded[pl.ds(base + STRIDE + 1, wide)]
        lower = padded[pl.ds(base - STRIDE - 1, wide)]
        for by, turn in shifts[1:]:
            code = float(4 * by + turn)
            upper = jnp.where(plus == code, padded[pl.ds(base + by * STRIDE + turn, wide)], upper)
            lower = jnp.where(minus == code, padded[pl.ds(base - by * STRIDE - turn, wide)], lower)
        value = coeff[pl.ds(base, wide)] * (
            here * here * (weight_plus * upper + weight_minus * lower)
            - 2.0 * weight_both * here * upper * lower
        )
        term[pl.ds(base, NDIR)] = value[:NDIR]
        term[pl.ds(base - 3, 3)] = value[NDIR - 3 : NDIR]
        term[pl.ds(base + NDIR, 3)] = value[:3]
        return carry

    lax.fori_loop(0, NFREQ, terms, 0, unroll=4)

    def gained(codes, at, code):
        rows = pl.ds(at, wide)
        return jnp.where(codes[rows] == code, term[rows], 0.0)

    def changes(f, carry):
        base = pl.multiple_of((f + 2) * STRIDE + LEAD, 8)
        value = padded[pl.ds(base, wide)] - 2.0 * term[pl.ds(base, wide)]
        for by, turn in shifts:
            code = float(4 * by + turn)
            value = value + gained(code_plus, base - by * STRIDE - turn, code)
            value = value + gained(code_minus, base + by * STRIDE + turn, code)
        out[pl.ds(f * NDIR, NDIR)] = value[:NDIR]
        return carry

    lax.fori_loop(0, NFREQ, changes, 0, unroll=4)
    high = (NFREQ + 1) * STRIDE + LEAD
    low = 2 * STRIDE + LEAD
    for turn in (1, 2, 3):
        code = float(4 + turn)
        out[BINS - NDIR :] = out[BINS - NDIR :] + gained(code_plus, high - turn, code)[:NDIR]
        out[:NDIR] = out[:NDIR] + gained(code_minus, low + turn, code)[:NDIR]

    for group in range(GROUPS):
        for step in range(STEPS):
            for row in range(BLOCKS):
                ghost_copy(group, step, row).wait_send()
                back_copy(group, step, row).wait_send()
        for shift in range(1, SPEC):
            spec_copy(group, shift).wait_send()


def direction_table():
    rows = np.arange(TROWS)
    values = []
    for start in (0, NDIR // 2):
        angle = ((rows + start) % NDIR) * (2.0 * math.pi / NDIR)
        values += [np.cos(angle), np.sin(angle)]
    return np.repeat(np.stack(values)[:, :, None], 128, axis=2).astype(np.float32)


def on_device(
    spectrum, normals, conn, send_nodes, step_weight, group_speed, dia_plus, dia_minus, dia_coeff
):
    vmem = pl.BlockSpec(memory_space=pltpu.VMEM)
    smem = pl.BlockSpec(memory_space=pltpu.SMEM)
    return pl.pallas_call(
        kernel,
        out_shape=jax.ShapeDtypeStruct((BINS, SLOT), f32),
        in_specs=[vmem, vmem, vmem, vmem, vmem, smem, vmem, vmem, vmem, vmem],
        out_specs=vmem,
        scratch_shapes=[
            pltpu.VMEM((GROUPS, SPEC, PAD, 128), f32),
            pltpu.VMEM((2 * PAD, OWN), bf16),
            pltpu.VMEM((GROUPS, PARTS, EXT), f8),
            pltpu.VMEM((OWN, BLOCKS * SLOT), bf16),
            pltpu.VMEM((EXT, 3 * ELEM), f8),
            pltpu.VMEM((EXT, 2 * ELEM), f8),
            pltpu.VMEM((3, TROWS, ELEM), f32),
            pltpu.VMEM((PARTS, 2 * CHUNK), f32),
            pltpu.VMEM((PARTS, 2 * CHUNK), f32),
            pltpu.VMEM((PARTS, 3 * CHUNK), f32),
            pltpu.VMEM((GROUPS, PARTS, 3 * ELEM), f8),
            pltpu.VMEM((GROUPS, PAD, OWN), f32),
            pltpu.VMEM((GROUPS, STEPS, BLOCKS, PAD, SLOT), f32),
            pltpu.VMEM((GROUPS, STEPS, BLOCKS, PAD, SLOT), f32),
            pltpu.VMEM((GROUPS, STEPS, BLOCKS, PAD, SLOT), f32),
            pltpu.VMEM((GROUPS, STEPS, BLOCKS, PAD, SLOT), f32),
            pltpu.VMEM((SPEC, ROWS + 6, 128), f32),
            pltpu.VMEM((BINS + 8, 128), f32),
            pltpu.VMEM((PADDED, 128), f32),
            pltpu.VMEM((PADDED, 128), f32),
            pltpu.VMEM((PADDED, 128), f32),
            pltpu.VMEM((PADDED, 128), f32),
            pltpu.VMEM((PADDED, 128), f32),
            pltpu.SemaphoreType.DMA((GROUPS, STEPS, 2, BLOCKS)),
            pltpu.SemaphoreType.DMA((GROUPS, STEPS, 2, BLOCKS)),
            pltpu.SemaphoreType.DMA((GROUPS, SPEC - 1)),
            pltpu.SemaphoreType.DMA((GROUPS, SPEC - 1)),
        ],
        compiler_params=pltpu.CompilerParams(
            collective_id=0, has_side_effects=True, vmem_limit_bytes=62 * 2**20
        ),
    )(
        spectrum,
        jnp.transpose(normals, (1, 0, 2)),
        conn,
        send_nodes,
        step_weight[None, :],
        group_speed,
        dia_plus,
        dia_minus,
        dia_coeff,
        jnp.asarray(direction_table()),
    )


def solution(mesh):
    in_specs = (
        P("spec", "dom"),
        P(None, None, "dom"),
        P(None, "dom"),
        P("dom", None, None),
        P("dom"),
        P(),
        P(),
        P(),
        P(),
    )
    out_specs = P(None, ("dom", "spec"))
    return jax.shard_map(
        on_device, mesh=mesh, in_specs=in_specs, out_specs=out_specs, check_vma=False
    )
```

```python
import functools
import math

import jax
import jax.numpy as jnp
import numpy as np
from jax import lax
from jax.experimental import pallas as pl
from jax.experimental.pallas import tpu as pltpu
from jax.sharding import PartitionSpec as P

NDIR = 36
NFREQ = 36
BINS = NDIR * NFREQ
STEPS = 2
DOM = 32
SPEC = 8
ROWS = BINS // SPEC
GROUPS = 2
MAIN = 80
TAIL = ROWS - 2 * MAIN
PAD = MAIN + 8
PARTS = 256
STEP8 = 16.0
OWN = 1024
SLOT = 128
BLOCKS = 4
EXT = OWN + BLOCKS * SLOT
ELEM = 2048
CHUNK = 256
CHUNKS = ELEM // CHUNK
TROWS = 88
OFFSETS = (-2, -1, 1, 2)
VALUE_LIMIT = 128.0
FLUX_LIMIT = 240.0
WHOLE = 1.5 * 2.0**23
STRIDE = 48
LEAD = 8
PADDED = (NFREQ + 4) * STRIDE + 8

weight_plus = 1.25 ** (-4)
weight_minus = 0.75 ** (-4)
weight_both = 0.9375 ** (-4)

MESH = pl.DeviceIdType.MESH
f32, bf16, f8 = jnp.float32, jnp.bfloat16, jnp.float8_e4m3fn


def split_two(value):
    high = value.astype(bf16).astype(f32)
    return jnp.concatenate([high, value - high], axis=0).astype(bf16)


def join_two(value):
    return value[:PAD] + value[PAD:]


def whole_number(value):
    return (value + WHOLE) - WHOLE


def three(value):
    first = whole_number(value)
    rest = (value - first.astype(f8).astype(f32)) * STEP8
    second = whole_number(rest)
    third = (rest - second.astype(f8).astype(f32)) * STEP8
    return first, second, third


def first_rows(value):
    return jnp.where(lax.broadcasted_iota(jnp.int32, value.shape, 0) < TAIL, value, 0.0)


def tail_parts(value):
    first, second, third = three(first_rows(value))
    return first + pltpu.roll(second, TAIL, 0) + pltpu.roll(third, 2 * TAIL, 0)


def join_tail(value):
    second, third = pltpu.roll(value, 8 - TAIL, 0), pltpu.roll(value, 8 - 2 * TAIL, 0)
    return first_rows(value + (second + third * (1 / STEP8)) * (1 / STEP8))


def split_three(value, group):
    zeros = jnp.zeros((8, value.shape[1]), f32)
    tail = tail_parts(value[MAIN:]) if group else zeros
    return jnp.concatenate([*three(value[:MAIN]), tail, zeros], axis=0).astype(f8)


def join_rows(value, first, size):
    at = [slice(part * MAIN + first, part * MAIN + first + size) for part in range(3)]
    return value[at[0]] + (value[at[1]] + value[at[2]] * (1 / STEP8)) * (1 / STEP8)


def join_three(value, group):
    zeros = jnp.zeros((8, value.shape[1]), f32)
    tail = join_tail(value[3 * MAIN : 3 * MAIN + 8]) if group else zeros
    return jnp.concatenate([join_rows(value, 0, MAIN), tail], axis=0)


def dot(left, right):
    return jnp.dot(left, right, preferred_element_type=f32)


def dot_t(left, right):
    return lax.dot_general(left, right, (((1,), (1,)), ((), ())), preferred_element_type=f32)


def lanes(index, size):
    return pl.ds(pl.multiple_of(index * size, size), size)


def kernel(
    spectrum,
    normals,
    conn,
    send_nodes,
    step_weight,
    group_speed,
    dia_plus,
    dia_minus,
    dia_coeff,
    table,
    out,
    energy,
    whole,
    parts,
    send_hot,
    corner_hot,
    edge_hot,
    edge_weight,
    even_diff,
    odd_diff,
    flux_parts,
    flux,
    own_sum,
    ghost_out,
    ghost_in,
    back_out,
    back_in,
    landing,
    linear,
    padded,
    term,
    code_plus,
    code_minus,
    coeff,
    halo_send,
    halo_recv,
    spec_send,
    spec_recv,
):
    dom = lax.axis_index("dom")
    spec = lax.axis_index("spec")

    barrier = pltpu.get_barrier_semaphore()
    for offset in OFFSETS:
        pl.semaphore_signal(
            barrier,
            inc=1,
            device_id={"dom": lax.rem(dom + offset + DOM, DOM), "spec": spec},
            device_id_type=MESH,
        )
    for shift in range(1, SPEC):
        pl.semaphore_signal(
            barrier,
            inc=1,
            device_id={"dom": dom, "spec": lax.rem(spec + shift, SPEC)},
            device_id_type=MESH,
        )

    for chunk in range(SPEC):
        at = slice(chunk * 128, (chunk + 1) * 128)
        energy[0, chunk, :MAIN] = spectrum[:MAIN, at]
        energy[0, chunk, MAIN:] = jnp.zeros((8, 128), f32)
        energy[1, chunk, : MAIN + TAIL] = spectrum[MAIN:, at]
        energy[1, chunk, MAIN + TAIL :] = jnp.zeros((8 - TAIL, 128), f32)
    flux_parts[3 * MAIN + 8 :] = jnp.zeros((PARTS - 3 * MAIN - 8, 3 * CHUNK), f32)

    for row in range(BLOCKS):
        index = jnp.broadcast_to(send_nodes[0, row : row + 1, :].astype(jnp.int16), (OWN, SLOT))
        node = lax.broadcasted_iota(jnp.int16, index.shape, 0)
        hot = jnp.where(node == index, bf16(1), bf16(0))
        send_hot[:, row * SLOT : (row + 1) * SLOT] = hot

    def halo_copy(group, step, back, block, source, target):
        return pltpu.make_async_remote_copy(
            src_ref=source.at[group, step, block],
            dst_ref=target.at[group, step, BLOCKS - 1 - block],
            send_sem=halo_send.at[group, step, back, block],
            recv_sem=halo_recv.at[group, step, back, block],
            device_id={"dom": lax.rem(dom + OFFSETS[block] + DOM, DOM), "spec": spec},
            device_id_type=MESH,
        )

    def ghost_copy(group, step, row):
        return halo_copy(group, step, 0, row, ghost_out, ghost_in)

    def back_copy(group, step, block):
        return halo_copy(group, step, 1, block, back_out, back_in)

    def make_ghosts(group, step):
        for chunk in range(SPEC):
            whole[:, chunk * 128 : (chunk + 1) * 128] = split_two(energy[group, chunk])
        pieces = join_two(dot(whole[...], send_hot[...]))
        for row in range(BLOCKS):
            ghost_out[group, step, row] = pieces[:, row * SLOT : (row + 1) * SLOT]

    def send_ghosts(group, step):
        for row in range(BLOCKS):
            ghost_copy(group, step, row).start()

    longest = normals[:, 0] * normals[:, 0] + normals[:, 1] * normals[:, 1]
    longest = jnp.sqrt(jnp.max(longest, axis=(0, 1), keepdims=True))
    flux_scale = (FLUX_LIMIT / (2 * VALUE_LIMIT)) / longest

    def edge_weights(chunk, carry):
        parity = lax.rem(spec, 2) == 0
        east = jnp.where(parity, table[0], table[2])
        north = jnp.where(parity, table[1], table[3])
        at = lanes(chunk, 128)
        k = [
            east * normals[corner, 0:1, at] + north * normals[corner, 1:2, at]
            for corner in range(3)
        ]
        into = [jnp.maximum(value, 0.0) for value in k]
        away = [jnp.maximum(-value, 0.0) for value in k]
        for edge in range(3):
            a, b = edge, (edge + 1) % 3
            sign = 1 if edge < 2 else -1
            edge_weight[2 * edge, :, at] = jnp.minimum(into[a], away[b]) * (flux_scale * sign)
            edge_weight[2 * edge + 1, :, at] = jnp.minimum(into[b], away[a]) * (flux_scale * -sign)
        return carry

    def build_hot(chunk, carry):
        one, minus, zero = [jnp.full((32, CHUNK), value, f32).astype(f8) for value in (1, -1, 0)]
        node = lax.broadcasted_iota(jnp.int32, (32, CHUNK), 0)
        nodes = [(node + first).astype(jnp.int8) for first in range(0, 128, 32)]
        corners = [conn[corner : corner + 1, lanes(chunk, CHUNK)] for corner in range(3)]
        for first in range(0, EXT, 128):
            local = [value - first for value in corners]
            local = [jnp.where((value >= 0) & (value < 128), value, -1) for value in local]
            local = [jnp.broadcast_to(value.astype(jnp.int8), (32, CHUNK)) for value in local]
            for quarter in range(4):
                rows = slice(first + 32 * quarter, first + 32 * quarter + 32)
                hits = [nodes[quarter] == value for value in local]
                for corner in range(3):
                    value = jnp.where(hits[corner], one, zero)
                    corner_hot[rows, lanes(chunk * 3 + corner, CHUNK)] = value
                for edge in range(2):
                    a, b = hits[edge], hits[edge + 1]
                    value = jnp.where(a, jnp.where(b, zero, one), jnp.where(b, minus, zero))
                    edge_hot[rows, lanes(chunk * 2 + edge, CHUNK)] = value
        return carry

    def edge_dot(group, chunk, target):
        target[...] = dot(parts[group], edge_hot[:, lanes(chunk, 2 * CHUNK)])

    def fluxes(group, chunk, diff):
        at = lanes(chunk, CHUNK)

        def corners(first, size, d01, d12):
            start = (group * MAIN + first) % (2 * NDIR)
            d02 = d01 + d12
            w01, w10, w12, w21, w20, w02 = [
                edge_weight[edge, start : start + size, at] for edge in range(6)
            ]
            return [w01 * d01 + w02 * d02, w12 * d12 + w10 * d01, w20 * d02 + w21 * d12]

        for first in range(0, MAIN, 16):
            edges = [
                join_rows(diff.at[:, edge * CHUNK : (edge + 1) * CHUNK], first, 16)
                for edge in range(2)
            ]
            for corner, value in enumerate(corners(first, 16, *edges)):
                column = slice(corner * CHUNK, (corner + 1) * CHUNK)
                for part, piece in enumerate(three(value)):
                    flux_parts[part * MAIN + first : part * MAIN + first + 16, column] = piece
        tail = slice(3 * MAIN, 3 * MAIN + 8)
        if group:
            edges = [
                join_tail(diff[tail, edge * CHUNK : (edge + 1) * CHUNK]) for edge in range(2)
            ]
            for corner, value in enumerate(corners(MAIN, 8, *edges)):
                flux_parts[tail, corner * CHUNK : (corner + 1) * CHUNK] = tail_parts(value)
        else:
            flux_parts[tail] = jnp.zeros((8, 3 * CHUNK), f32)
        flux[group, :, lanes(chunk, 3 * CHUNK)] = flux_parts[...].astype(f8)

    def gather(group):
        def pair(index, carry):
            edge_dot(group, 2 * index + 1, odd_diff)
            fluxes(group, 2 * index, even_diff)
            edge_dot(group, 2 * index + 2, even_diff)
            fluxes(group, 2 * index + 1, odd_diff)
            return carry

        edge_dot(group, 0, even_diff)
        lax.fori_loop(0, CHUNKS // 2 - 1, pair, 0)
        edge_dot(group, CHUNKS - 1, odd_diff)
        fluxes(group, CHUNKS - 2, even_diff)
        fluxes(group, CHUNKS - 1, odd_diff)

    first_bin = spec * ROWS
    first_freq = first_bin // NDIR
    speeds = []
    for group in range(GROUPS):
        start = first_bin - first_freq * NDIR + group * MAIN
        row = lax.broadcasted_iota(jnp.int32, (PAD, 128), 0) + start
        speed = jnp.full((PAD, 128), group_speed[first_freq], f32)
        for later in range(1, 6):
            value = group_speed[jnp.minimum(first_freq + later, NFREQ - 1)]
            speed = jnp.where(row >= later * NDIR, value, speed)
        speeds.append(speed)

    unscale = [None] * GROUPS

    def ready(group, step):
        for row in range(BLOCKS):
            ghost_copy(group, step, row).wait_recv()
        chunks = [energy.at[group, chunk] for chunk in range(SPEC)]
        chunks += [ghost_in.at[group, step, block] for block in range(BLOCKS)]
        most = least = chunks[0][:MAIN]
        for ref in chunks:
            most = jnp.maximum(most, ref[:MAIN])
            least = jnp.minimum(least, ref[:MAIN])
            if group:
                tail = ref[MAIN : MAIN + TAIL]
                most = jnp.maximum(most, jnp.max(tail, axis=0, keepdims=True))
                least = jnp.minimum(least, jnp.min(tail, axis=0, keepdims=True))
        most = jnp.max(most, axis=(0, 1), keepdims=True)
        least = jnp.min(least, axis=(0, 1), keepdims=True)
        middle = 0.5 * (most + least)
        reach = jnp.maximum(0.5001 * (most - least), 1e-30)
        scale = VALUE_LIMIT / reach
        unscale[group] = reach * longest * (2 / FLUX_LIMIT)
        for chunk, ref in enumerate(chunks):
            value = (ref[...] - middle) * scale
            parts[group, :, chunk * 128 : (chunk + 1) * 128] = split_three(value, group)

    def ghost_scatter(group, step):
        total = dot_t(flux[group], corner_hot[OWN:, :])
        total = join_three(total, group) * unscale[group]
        for block in range(BLOCKS):
            back_out[group, step, block] = total[:, block * SLOT : (block + 1) * SLOT]
            back_copy(group, step, block).start()

    def own_scatter(group):
        def half(index, carry):
            rows = lanes(index, 512)
            own_sum[group, :, rows] = join_three(dot_t(flux[group], corner_hot[rows, :]), group)
            return carry

        lax.fori_loop(0, 2, half, 0)

    def update(group, step):
        for block in range(BLOCKS):
            back_copy(group, step, block).wait_recv()
        returned = [split_two(back_in[group, step, row]) for row in range(BLOCKS)]
        returned = jnp.concatenate(returned, axis=1)
        for half in range(2):
            at = slice(half * 512, (half + 1) * 512)
            total = own_sum[group, :, at] * unscale[group]
            total = total + join_two(dot_t(returned, send_hot[at, :]))
            for quarter in range(4):
                chunk = half * 4 + quarter
                weight = speeds[group] * step_weight[:, chunk * 128 : (chunk + 1) * 128]
                change = weight * total[:, quarter * 128 : (quarter + 1) * 128]
                energy[group, chunk] = energy[group, chunk] - change

    def spec_copy(group, shift):
        to = lax.rem(spec + shift, SPEC)
        count = MAIN + TAIL * group
        return pltpu.make_async_remote_copy(
            src_ref=energy.at[group, to, pl.ds(0, count)],
            dst_ref=landing.at[spec, pl.ds(group * MAIN, count)],
            send_sem=spec_send.at[group, shift - 1],
            recv_sem=spec_recv.at[group, shift - 1],
            device_id={"dom": dom, "spec": to},
            device_id_type=MESH,
        )

    def spread(group):
        for shift in (4, 3, 5, 2, 6, 1, 7):
            spec_copy(group, shift).start()
        count = MAIN + TAIL * group
        landing[spec, pl.ds(group * MAIN, count)] = energy[group, spec, :count]

    for group in range(GROUPS):
        make_ghosts(group, 0)
    lax.fori_loop(0, CHUNKS, build_hot, 0)
    lax.fori_loop(0, ELEM // 128, edge_weights, 0)
    pl.semaphore_wait(barrier, BLOCKS + SPEC - 1)
    for group in range(GROUPS):
        send_ghosts(group, 0)

    for group in range(GROUPS):
        ready(group, 0)
        gather(group)
        ghost_scatter(group, 0)
    for group in range(GROUPS):
        own_scatter(group)
        update(group, 0)
        make_ghosts(group, 1)
        send_ghosts(group, 1)
    ready(0, 1)
    gather(0)
    ghost_scatter(0, 1)
    own_scatter(0)
    ready(1, 1)
    gather(1)
    update(0, 1)
    spread(0)
    ghost_scatter(1, 1)
    own_scatter(1)
    update(1, 1)
    spread(1)

    def partner_code(partner, first, sign):
        bin_ = lax.broadcasted_iota(jnp.int32, (1, 128), 1).astype(f32) + first
        freq = jnp.floor((bin_ + 0.5) * (1.0 / NDIR))
        partner = partner.astype(f32)
        other = jnp.floor((partner + 0.5) * (1.0 / NDIR))
        turn = sign * ((partner - NDIR * other) - (bin_ - NDIR * freq))
        turn = jnp.where(turn < 0, turn + NDIR, turn)
        return 4 * jnp.maximum(sign * (other - freq), 1.0) + turn

    def to_column(value, rule):
        for first in range(0, BINS, 128):
            start = min(first, BINS - 128)
            piece = rule(value[start : start + 128].reshape(1, 128), float(start))
            linear[start : start + 128] = jnp.broadcast_to(piece, (128, 128)).T

    def to_padded(target):
        def one(f, carry):
            base = pl.multiple_of((f + 2) * STRIDE, 8)
            value = linear[pl.ds(f * NDIR, NDIR)]
            target[pl.ds(base + LEAD, NDIR)] = value
            target[pl.ds(base + LEAD - 3, 3)] = value[NDIR - 3 :]
            target[pl.ds(base + LEAD + NDIR, 3)] = value[:3]
            return carry

        lax.fori_loop(0, NFREQ, one, 0)

    for target, value, rule in (
        (code_plus, dia_plus, functools.partial(partner_code, sign=1.0)),
        (code_minus, dia_minus, functools.partial(partner_code, sign=-1.0)),
        (coeff, dia_coeff, lambda value, first: value),
    ):
        target[...] = jnp.zeros((PADDED, 128), f32)
        to_column(value, rule)
        to_padded(target)

    for group in range(GROUPS):
        for shift in range(1, SPEC):
            source = lax.rem(spec + SPEC - shift, SPEC)
            place = landing.at[source, pl.ds(group * MAIN, MAIN + TAIL * group)]
            pltpu.make_async_remote_copy(
                src_ref=place,
                dst_ref=place,
                send_sem=spec_send.at[group, shift - 1],
                recv_sem=spec_recv.at[group, shift - 1],
                device_id={"dom": dom, "spec": source},
                device_id_type=MESH,
            ).wait_recv()

    half = NDIR // 2
    for source in range(SPEC):
        for piece in range(ROWS // half):
            f, second = divmod(source * (ROWS // half) + piece, 2)
            base = (f + 2) * STRIDE + LEAD
            value = landing[source, piece * half : (piece + 1) * half]
            padded[base + second * half : base + (second + 1) * half] = value
            if second:
                padded[base - 3 : base] = value[half - 3 :]
            else:
                padded[base + NDIR : base + NDIR + 3] = value[:3]
    for block in range(2):
        padded[block * STRIDE : (block + 1) * STRIDE] = padded[2 * STRIDE : 3 * STRIDE]
        last = (NFREQ + 2 + block) * STRIDE
        padded[last : last + STRIDE] = padded[(NFREQ + 1) * STRIDE : (NFREQ + 2) * STRIDE]

    wide = 40
    shifts = [(by, turn) for by in (1, 2) for turn in (1, 2, 3)]

    def terms(f, carry):
        base = pl.multiple_of((f + 2) * STRIDE + LEAD, 8)
        here = padded[pl.ds(base, wide)]
        plus = code_plus[pl.ds(base, wide)]
        minus = code_minus[pl.ds(base, wide)]
        upper = padded[pl.ds(base + STRIDE + 1, wide)]
        lower = padded[pl.ds(base - STRIDE - 1, wide)]
        for by, turn in shifts[1:]:
            code = float(4 * by + turn)
            upper = jnp.where(plus == code, padded[pl.ds(base + by * STRIDE + turn, wide)], upper)
            lower = jnp.where(minus == code, padded[pl.ds(base - by * STRIDE - turn, wide)], lower)
        value = coeff[pl.ds(base, wide)] * (
            here * here * (weight_plus * upper + weight_minus * lower)
            - 2.0 * weight_both * here * upper * lower
        )
        term[pl.ds(base, NDIR)] = value[:NDIR]
        term[pl.ds(base - 3, 3)] = value[NDIR - 3 : NDIR]
        term[pl.ds(base + NDIR, 3)] = value[:3]
        return carry

    lax.fori_loop(0, NFREQ, terms, 0, unroll=4)

    def gained(codes, at, code):
        rows = pl.ds(at, wide)
        return jnp.where(codes[rows] == code, term[rows], 0.0)

    def changes(f, carry):
        base = pl.multiple_of((f + 2) * STRIDE + LEAD, 8)
        value = padded[pl.ds(base, wide)] - 2.0 * term[pl.ds(base, wide)]
        for by, turn in shifts:
            code = float(4 * by + turn)
            value = value + gained(code_plus, base - by * STRIDE - turn, code)
            value = value + gained(code_minus, base + by * STRIDE + turn, code)
        out[pl.ds(f * NDIR, NDIR)] = value[:NDIR]
        return carry

    lax.fori_loop(0, NFREQ, changes, 0, unroll=4)
    high = (NFREQ + 1) * STRIDE + LEAD
    low = 2 * STRIDE + LEAD
    for turn in (1, 2, 3):
        code = float(4 + turn)
        out[BINS - NDIR :] = out[BINS - NDIR :] + gained(code_plus, high - turn, code)[:NDIR]
        out[:NDIR] = out[:NDIR] + gained(code_minus, low + turn, code)[:NDIR]

    for group in range(GROUPS):
        for step in range(STEPS):
            for row in range(BLOCKS):
                ghost_copy(group, step, row).wait_send()
                back_copy(group, step, row).wait_send()
        for shift in range(1, SPEC):
            spec_copy(group, shift).wait_send()


def direction_table():
    rows = np.arange(TROWS)
    values = []
    for start in (0, NDIR // 2):
        angle = ((rows + start) % NDIR) * (2.0 * math.pi / NDIR)
        values += [np.cos(angle), np.sin(angle)]
    return np.repeat(np.stack(values)[:, :, None], 128, axis=2).astype(np.float32)


def on_device(
    spectrum, normals, conn, send_nodes, step_weight, group_speed, dia_plus, dia_minus, dia_coeff
):
    vmem = pl.BlockSpec(memory_space=pltpu.VMEM)
    smem = pl.BlockSpec(memory_space=pltpu.SMEM)
    return pl.pallas_call(
        kernel,
        out_shape=jax.ShapeDtypeStruct((BINS, SLOT), f32),
        in_specs=[vmem, vmem, vmem, vmem, vmem, smem, vmem, vmem, vmem, vmem],
        out_specs=vmem,
        scratch_shapes=[
            pltpu.VMEM((GROUPS, SPEC, PAD, 128), f32),
            pltpu.VMEM((2 * PAD, OWN), bf16),
            pltpu.VMEM((GROUPS, PARTS, EXT), f8),
            pltpu.VMEM((OWN, BLOCKS * SLOT), bf16),
            pltpu.VMEM((EXT, 3 * ELEM), f8),
            pltpu.VMEM((EXT, 2 * ELEM), f8),
            pltpu.VMEM((6, TROWS, ELEM), f32),
            pltpu.VMEM((PARTS, 2 * CHUNK), f32),
            pltpu.VMEM((PARTS, 2 * CHUNK), f32),
            pltpu.VMEM((PARTS, 3 * CHUNK), f32),
            pltpu.VMEM((GROUPS, PARTS, 3 * ELEM), f8),
            pltpu.VMEM((GROUPS, PAD, OWN), f32),
            pltpu.VMEM((GROUPS, STEPS, BLOCKS, PAD, SLOT), f32),
            pltpu.VMEM((GROUPS, STEPS, BLOCKS, PAD, SLOT), f32),
            pltpu.VMEM((GROUPS, STEPS, BLOCKS, PAD, SLOT), f32),
            pltpu.VMEM((GROUPS, STEPS, BLOCKS, PAD, SLOT), f32),
            pltpu.VMEM((SPEC, ROWS + 6, 128), f32),
            pltpu.VMEM((BINS + 8, 128), f32),
            pltpu.VMEM((PADDED, 128), f32),
            pltpu.VMEM((PADDED, 128), f32),
            pltpu.VMEM((PADDED, 128), f32),
            pltpu.VMEM((PADDED, 128), f32),
            pltpu.VMEM((PADDED, 128), f32),
            pltpu.SemaphoreType.DMA((GROUPS, STEPS, 2, BLOCKS)),
            pltpu.SemaphoreType.DMA((GROUPS, STEPS, 2, BLOCKS)),
            pltpu.SemaphoreType.DMA((GROUPS, SPEC - 1)),
            pltpu.SemaphoreType.DMA((GROUPS, SPEC - 1)),
        ],
        compiler_params=pltpu.CompilerParams(
            collective_id=0, has_side_effects=True, vmem_limit_bytes=62 * 2**20
        ),
    )(
        spectrum,
        jnp.transpose(normals, (1, 0, 2)),
        conn,
        send_nodes,
        step_weight[None, :],
        group_speed,
        dia_plus,
        dia_minus,
        dia_coeff,
        jnp.asarray(direction_table()),
    )


def solution(mesh):
    in_specs = (
        P("spec", "dom"),
        P(None, None, "dom"),
        P(None, "dom"),
        P("dom", None, None),
        P("dom"),
        P(),
        P(),
        P(),
        P(),
    )
    out_specs = P(None, ("dom", "spec"))
    return jax.shard_map(
        on_device, mesh=mesh, in_specs=in_specs, out_specs=out_specs, check_vma=False
    )
```

```python
import functools
import math

import jax
import jax.numpy as jnp
import numpy as np
from jax import lax
from jax.experimental import pallas as pl
from jax.experimental.pallas import tpu as pltpu
from jax.sharding import PartitionSpec as P

NDIR = 36
NFREQ = 36
BINS = NDIR * NFREQ
STEPS = 2
DOM = 32
SPEC = 8
ROWS = BINS // SPEC
GROUPS = 2
MAIN = 80
TAIL = ROWS - 2 * MAIN
PAD = MAIN + 8
PARTS = 256
STEP8 = 16.0
OWN = 1024
SLOT = 128
BLOCKS = 4
EXT = OWN + BLOCKS * SLOT
ELEM = 2048
CHUNK = 256
CHUNKS = ELEM // CHUNK
TROWS = 88
OFFSETS = (-2, -1, 1, 2)
VALUE_LIMIT = 128.0
FLUX_LIMIT = 240.0
WHOLE = 1.5 * 2.0**23
STRIDE = 48
LEAD = 8
PADDED = (NFREQ + 4) * STRIDE + 8

weight_plus = 1.25 ** (-4)
weight_minus = 0.75 ** (-4)
weight_both = 0.9375 ** (-4)

MESH = pl.DeviceIdType.MESH
f32, bf16, f8 = jnp.float32, jnp.bfloat16, jnp.float8_e4m3fn


def split_two(value):
    high = value.astype(bf16).astype(f32)
    return jnp.concatenate([high, value - high], axis=0).astype(bf16)


def join_two(value):
    return value[:PAD] + value[PAD:]


def whole_number(value):
    return (value + WHOLE) - WHOLE


def three(value):
    first = whole_number(value)
    rest = (value - first.astype(f8).astype(f32)) * STEP8
    second = whole_number(rest)
    third = (rest - second.astype(f8).astype(f32)) * STEP8
    return first, second, third


def first_rows(value):
    return jnp.where(lax.broadcasted_iota(jnp.int32, value.shape, 0) < TAIL, value, 0.0)


def tail_parts(value):
    first, second, third = three(first_rows(value))
    return first + pltpu.roll(second, TAIL, 0) + pltpu.roll(third, 2 * TAIL, 0)


def join_tail(value):
    second, third = pltpu.roll(value, 8 - TAIL, 0), pltpu.roll(value, 8 - 2 * TAIL, 0)
    return first_rows(value + (second + third * (1 / STEP8)) * (1 / STEP8))


def split_three(value, group):
    zeros = jnp.zeros((8, value.shape[1]), f32)
    tail = tail_parts(value[MAIN:]) if group else zeros
    return jnp.concatenate([*three(value[:MAIN]), tail, zeros], axis=0).astype(f8)


def join_rows(value, first, size):
    at = [slice(part * MAIN + first, part * MAIN + first + size) for part in range(3)]
    return value[at[0]] + (value[at[1]] + value[at[2]] * (1 / STEP8)) * (1 / STEP8)


def join_three(value, group):
    zeros = jnp.zeros((8, value.shape[1]), f32)
    tail = join_tail(value[3 * MAIN : 3 * MAIN + 8]) if group else zeros
    return jnp.concatenate([join_rows(value, 0, MAIN), tail], axis=0)


def dot(left, right):
    return jnp.dot(left, right, preferred_element_type=f32)


def dot_t(left, right):
    return lax.dot_general(left, right, (((1,), (1,)), ((), ())), preferred_element_type=f32)


def lanes(index, size):
    return pl.ds(pl.multiple_of(index * size, size), size)


def kernel(
    spectrum,
    normals,
    conn,
    send_nodes,
    step_weight,
    group_speed,
    dia_plus,
    dia_minus,
    dia_coeff,
    table,
    out,
    energy,
    whole,
    parts,
    send_hot,
    corner_hot,
    edge_hot,
    edge_weight,
    even_diff,
    odd_diff,
    flux_parts,
    flux,
    own_sum,
    ghost_out,
    ghost_in,
    back_out,
    back_in,
    landing,
    linear,
    padded,
    term,
    code_plus,
    code_minus,
    coeff,
    halo_send,
    halo_recv,
    spec_send,
    spec_recv,
):
    dom = lax.axis_index("dom")
    spec = lax.axis_index("spec")

    barrier = pltpu.get_barrier_semaphore()
    for offset in OFFSETS:
        pl.semaphore_signal(
            barrier,
            inc=1,
            device_id={"dom": lax.rem(dom + offset + DOM, DOM), "spec": spec},
            device_id_type=MESH,
        )
    for shift in range(1, SPEC):
        pl.semaphore_signal(
            barrier,
            inc=1,
            device_id={"dom": dom, "spec": lax.rem(spec + shift, SPEC)},
            device_id_type=MESH,
        )

    for chunk in range(SPEC):
        at = slice(chunk * 128, (chunk + 1) * 128)
        energy[0, chunk, :MAIN] = spectrum[:MAIN, at]
        energy[0, chunk, MAIN:] = jnp.zeros((8, 128), f32)
        energy[1, chunk, : MAIN + TAIL] = spectrum[MAIN:, at]
        energy[1, chunk, MAIN + TAIL :] = jnp.zeros((8 - TAIL, 128), f32)
    flux_parts[3 * MAIN + 8 :] = jnp.zeros((PARTS - 3 * MAIN - 8, 3 * CHUNK), f32)

    for row in range(BLOCKS):
        index = jnp.broadcast_to(send_nodes[0, row : row + 1, :].astype(jnp.int16), (OWN, SLOT))
        node = lax.broadcasted_iota(jnp.int16, index.shape, 0)
        hot = jnp.where(node == index, bf16(1), bf16(0))
        send_hot[:, row * SLOT : (row + 1) * SLOT] = hot

    def halo_copy(group, step, back, block, source, target):
        return pltpu.make_async_remote_copy(
            src_ref=source.at[group, step, block],
            dst_ref=target.at[group, step, BLOCKS - 1 - block],
            send_sem=halo_send.at[group, step, back, block],
            recv_sem=halo_recv.at[group, step, back, block],
            device_id={"dom": lax.rem(dom + OFFSETS[block] + DOM, DOM), "spec": spec},
            device_id_type=MESH,
        )

    def ghost_copy(group, step, row):
        return halo_copy(group, step, 0, row, ghost_out, ghost_in)

    def back_copy(group, step, block):
        return halo_copy(group, step, 1, block, back_out, back_in)

    def make_ghosts(group, step):
        for chunk in range(SPEC):
            whole[:, chunk * 128 : (chunk + 1) * 128] = split_two(energy[group, chunk])
        pieces = join_two(dot(whole[...], send_hot[...]))
        for row in range(BLOCKS):
            ghost_out[group, step, row] = pieces[:, row * SLOT : (row + 1) * SLOT]

    def send_ghosts(group, step):
        for row in range(BLOCKS):
            ghost_copy(group, step, row).start()

    longest = normals[:, 0] * normals[:, 0] + normals[:, 1] * normals[:, 1]
    longest = jnp.sqrt(jnp.max(longest, axis=(0, 1), keepdims=True))
    flux_scale = (FLUX_LIMIT / (2 * VALUE_LIMIT)) / longest

    def edge_weights(chunk, carry):
        parity = lax.rem(spec, 2) == 0
        east = jnp.where(parity, table[0], table[2])
        north = jnp.where(parity, table[1], table[3])
        at = lanes(chunk, 128)
        k = [
            east * normals[corner, 0:1, at] + north * normals[corner, 1:2, at]
            for corner in range(3)
        ]
        into = [jnp.maximum(value, 0.0) for value in k]
        away = [jnp.maximum(-value, 0.0) for value in k]
        for edge in range(3):
            a, b = edge, (edge + 1) % 3
            sign = 1 if edge < 2 else -1
            edge_weight[2 * edge, :, at] = jnp.minimum(into[a], away[b]) * (flux_scale * sign)
            edge_weight[2 * edge + 1, :, at] = jnp.minimum(into[b], away[a]) * (flux_scale * -sign)
        return carry

    def build_hot(chunk, carry):
        one, minus, zero = [jnp.full((32, CHUNK), value, f32).astype(f8) for value in (1, -1, 0)]
        node = lax.broadcasted_iota(jnp.int32, (32, CHUNK), 0)
        nodes = [(node + first).astype(jnp.int8) for first in range(0, 128, 32)]
        corners = [conn[corner : corner + 1, lanes(chunk, CHUNK)] for corner in range(3)]
        for first in range(0, EXT, 128):
            local = [value - first for value in corners]
            local = [jnp.where((value >= 0) & (value < 128), value, -1) for value in local]
            local = [jnp.broadcast_to(value.astype(jnp.int8), (32, CHUNK)) for value in local]
            for quarter in range(4):
                rows = slice(first + 32 * quarter, first + 32 * quarter + 32)
                hits = [nodes[quarter] == value for value in local]
                for corner in range(3):
                    value = jnp.where(hits[corner], one, zero)
                    corner_hot[rows, lanes(chunk * 3 + corner, CHUNK)] = value
                for edge in range(2):
                    a, b = hits[edge], hits[edge + 1]
                    value = jnp.where(a, jnp.where(b, zero, one), jnp.where(b, minus, zero))
                    edge_hot[rows, lanes(chunk * 2 + edge, CHUNK)] = value
        return carry

    def edge_dot(group, chunk, target):
        target[...] = dot(parts[group], edge_hot[:, lanes(chunk, 2 * CHUNK)])

    def fluxes(group, chunk, diff):
        at = lanes(chunk, CHUNK)

        def corners(first, size, d01, d12):
            start = (group * MAIN + first) % (2 * NDIR)
            d02 = d01 + d12
            w01, w10, w12, w21, w20, w02 = [
                edge_weight[edge, start : start + size, at] for edge in range(6)
            ]
            return [w01 * d01 + w02 * d02, w12 * d12 + w10 * d01, w20 * d02 + w21 * d12]

        for first in range(0, MAIN, 16):
            edges = [
                join_rows(diff.at[:, edge * CHUNK : (edge + 1) * CHUNK], first, 16)
                for edge in range(2)
            ]
            for corner, value in enumerate(corners(first, 16, *edges)):
                column = slice(corner * CHUNK, (corner + 1) * CHUNK)
                for part, piece in enumerate(three(value)):
                    flux_parts[part * MAIN + first : part * MAIN + first + 16, column] = piece
        tail = slice(3 * MAIN, 3 * MAIN + 8)
        if group:
            edges = [
                join_tail(diff[tail, edge * CHUNK : (edge + 1) * CHUNK]) for edge in range(2)
            ]
            for corner, value in enumerate(corners(MAIN, 8, *edges)):
                flux_parts[tail, corner * CHUNK : (corner + 1) * CHUNK] = tail_parts(value)
        else:
            flux_parts[tail] = jnp.zeros((8, 3 * CHUNK), f32)
        flux[group, :, lanes(chunk, 3 * CHUNK)] = flux_parts[...].astype(f8)

    def gather(group):
        def pair(index, carry):
            edge_dot(group, 2 * index + 1, odd_diff)
            fluxes(group, 2 * index, even_diff)
            edge_dot(group, 2 * index + 2, even_diff)
            fluxes(group, 2 * index + 1, odd_diff)
            return carry

        edge_dot(group, 0, even_diff)
        lax.fori_loop(0, CHUNKS // 2 - 1, pair, 0)
        edge_dot(group, CHUNKS - 1, odd_diff)
        fluxes(group, CHUNKS - 2, even_diff)
        fluxes(group, CHUNKS - 1, odd_diff)

    first_bin = spec * ROWS
    first_freq = first_bin // NDIR
    speeds = []
    for group in range(GROUPS):
        start = first_bin - first_freq * NDIR + group * MAIN
        row = lax.broadcasted_iota(jnp.int32, (PAD, 128), 0) + start
        speed = jnp.full((PAD, 128), group_speed[first_freq], f32)
        for later in range(1, 6):
            value = group_speed[jnp.minimum(first_freq + later, NFREQ - 1)]
            speed = jnp.where(row >= later * NDIR, value, speed)
        speeds.append(speed)

    unscale = [None] * GROUPS

    def ready(group, step):
        for row in range(BLOCKS):
            ghost_copy(group, step, row).wait_recv()
        chunks = [energy.at[group, chunk] for chunk in range(SPEC)]
        chunks += [ghost_in.at[group, step, block] for block in range(BLOCKS)]
        most = least = chunks[0][:MAIN]
        for ref in chunks:
            most = jnp.maximum(most, ref[:MAIN])
            least = jnp.minimum(least, ref[:MAIN])
            if group:
                tail = ref[MAIN : MAIN + TAIL]
                most = jnp.maximum(most, jnp.max(tail, axis=0, keepdims=True))
                least = jnp.minimum(least, jnp.min(tail, axis=0, keepdims=True))
        most = jnp.max(most, axis=(0, 1), keepdims=True)
        least = jnp.min(least, axis=(0, 1), keepdims=True)
        middle = 0.5 * (most + least)
        reach = jnp.maximum(0.5001 * (most - least), 1e-30)
        scale = VALUE_LIMIT / reach
        unscale[group] = reach * longest * (2 / FLUX_LIMIT)
        for chunk, ref in enumerate(chunks):
            value = (ref[...] - middle) * scale
            parts[group, :, chunk * 128 : (chunk + 1) * 128] = split_three(value, group)

    def ghost_scatter(group, step):
        total = dot_t(flux[group], corner_hot[OWN:, :])
        total = join_three(total, group) * unscale[group]
        for block in range(BLOCKS):
            back_out[group, step, block] = total[:, block * SLOT : (block + 1) * SLOT]
            back_copy(group, step, block).start()

    def own_scatter(group):
        def half(index, carry):
            rows = lanes(index, 512)
            own_sum[group, :, rows] = join_three(dot_t(flux[group], corner_hot[rows, :]), group)
            return carry

        lax.fori_loop(0, 2, half, 0)

    def update(group, step):
        for block in range(BLOCKS):
            back_copy(group, step, block).wait_recv()
        returned = [split_two(back_in[group, step, row]) for row in range(BLOCKS)]
        returned = jnp.concatenate(returned, axis=1)
        for half in range(2):
            at = slice(half * 512, (half + 1) * 512)
            total = own_sum[group, :, at] * unscale[group]
            total = total + join_two(dot_t(returned, send_hot[at, :]))
            for quarter in range(4):
                chunk = half * 4 + quarter
                weight = speeds[group] * step_weight[:, chunk * 128 : (chunk + 1) * 128]
                change = weight * total[:, quarter * 128 : (quarter + 1) * 128]
                energy[group, chunk] = energy[group, chunk] - change

    def spec_copy(group, shift):
        to = lax.rem(spec + shift, SPEC)
        count = MAIN + TAIL * group
        return pltpu.make_async_remote_copy(
            src_ref=energy.at[group, to, pl.ds(0, count)],
            dst_ref=landing.at[spec, pl.ds(group * MAIN, count)],
            send_sem=spec_send.at[group, shift - 1],
            recv_sem=spec_recv.at[group, shift - 1],
            device_id={"dom": dom, "spec": to},
            device_id_type=MESH,
        )

    def spread(group):
        for shift in (4, 3, 5, 2, 6, 1, 7):
            spec_copy(group, shift).start()
        count = MAIN + TAIL * group
        landing[spec, pl.ds(group * MAIN, count)] = energy[group, spec, :count]

    for group in range(GROUPS):
        make_ghosts(group, 0)
    lax.fori_loop(0, 2, build_hot, 0)
    pl.semaphore_wait(barrier, BLOCKS + SPEC - 1)
    for group in range(GROUPS):
        send_ghosts(group, 0)
    lax.fori_loop(2, CHUNKS, build_hot, 0)
    lax.fori_loop(0, ELEM // 128, edge_weights, 0)

    for group in range(GROUPS):
        ready(group, 0)
        gather(group)
        ghost_scatter(group, 0)
    for group in range(GROUPS):
        own_scatter(group)
        update(group, 0)
        make_ghosts(group, 1)
        send_ghosts(group, 1)
    ready(0, 1)
    gather(0)
    ghost_scatter(0, 1)
    own_scatter(0)
    ready(1, 1)
    gather(1)
    update(0, 1)
    spread(0)
    ghost_scatter(1, 1)
    own_scatter(1)
    update(1, 1)
    spread(1)

    def partner_code(partner, first, sign):
        bin_ = lax.broadcasted_iota(jnp.int32, (1, 128), 1).astype(f32) + first
        freq = jnp.floor((bin_ + 0.5) * (1.0 / NDIR))
        partner = partner.astype(f32)
        other = jnp.floor((partner + 0.5) * (1.0 / NDIR))
        turn = sign * ((partner - NDIR * other) - (bin_ - NDIR * freq))
        turn = jnp.where(turn < 0, turn + NDIR, turn)
        return 4 * jnp.maximum(sign * (other - freq), 1.0) + turn

    def to_column(value, rule):
        for first in range(0, BINS, 128):
            start = min(first, BINS - 128)
            piece = rule(value[start : start + 128].reshape(1, 128), float(start))
            linear[start : start + 128] = jnp.broadcast_to(piece, (128, 128)).T

    def to_padded(target):
        def one(f, carry):
            base = pl.multiple_of((f + 2) * STRIDE, 8)
            value = linear[pl.ds(f * NDIR, NDIR)]
            target[pl.ds(base + LEAD, NDIR)] = value
            target[pl.ds(base + LEAD - 3, 3)] = value[NDIR - 3 :]
            target[pl.ds(base + LEAD + NDIR, 3)] = value[:3]
            return carry

        lax.fori_loop(0, NFREQ, one, 0)

    for target, value, rule in (
        (code_plus, dia_plus, functools.partial(partner_code, sign=1.0)),
        (code_minus, dia_minus, functools.partial(partner_code, sign=-1.0)),
        (coeff, dia_coeff, lambda value, first: value),
    ):
        target[...] = jnp.zeros((PADDED, 128), f32)
        to_column(value, rule)
        to_padded(target)

    half = NDIR // 2
    early = MAIN // half

    def place_pieces(first, last):
        for source in range(SPEC):
            for piece in range(first, last):
                f, second = divmod(source * (ROWS // half) + piece, 2)
                base = (f + 2) * STRIDE + LEAD
                value = landing[source, piece * half : (piece + 1) * half]
                padded[base + second * half : base + (second + 1) * half] = value
                if second:
                    padded[base - 3 : base] = value[half - 3 :]
                else:
                    padded[base + NDIR : base + NDIR + 3] = value[:3]

    for group in range(GROUPS):
        for shift in range(1, SPEC):
            source = lax.rem(spec + SPEC - shift, SPEC)
            place = landing.at[source, pl.ds(group * MAIN, MAIN + TAIL * group)]
            pltpu.make_async_remote_copy(
                src_ref=place,
                dst_ref=place,
                send_sem=spec_send.at[group, shift - 1],
                recv_sem=spec_recv.at[group, shift - 1],
                device_id={"dom": dom, "spec": source},
                device_id_type=MESH,
            ).wait_recv()
        place_pieces(*((early, ROWS // half) if group else (0, early)))

    for block in range(2):
        padded[block * STRIDE : (block + 1) * STRIDE] = padded[2 * STRIDE : 3 * STRIDE]
        last = (NFREQ + 2 + block) * STRIDE
        padded[last : last + STRIDE] = padded[(NFREQ + 1) * STRIDE : (NFREQ + 2) * STRIDE]

    wide = 40
    shifts = [(by, turn) for by in (1, 2) for turn in (1, 2, 3)]

    def terms(f, carry):
        base = pl.multiple_of((f + 2) * STRIDE + LEAD, 8)
        here = padded[pl.ds(base, wide)]
        plus = code_plus[pl.ds(base, wide)]
        minus = code_minus[pl.ds(base, wide)]
        upper = padded[pl.ds(base + STRIDE + 1, wide)]
        lower = padded[pl.ds(base - STRIDE - 1, wide)]
        for by, turn in shifts[1:]:
            code = float(4 * by + turn)
            upper = jnp.where(plus == code, padded[pl.ds(base + by * STRIDE + turn, wide)], upper)
            lower = jnp.where(minus == code, padded[pl.ds(base - by * STRIDE - turn, wide)], lower)
        value = coeff[pl.ds(base, wide)] * (
            here * here * (weight_plus * upper + weight_minus * lower)
            - 2.0 * weight_both * here * upper * lower
        )
        term[pl.ds(base, NDIR)] = value[:NDIR]
        term[pl.ds(base - 3, 3)] = value[NDIR - 3 : NDIR]
        term[pl.ds(base + NDIR, 3)] = value[:3]
        return carry

    lax.fori_loop(0, NFREQ, terms, 0, unroll=4)

    def gained(codes, at, code):
        rows = pl.ds(at, wide)
        return jnp.where(codes[rows] == code, term[rows], 0.0)

    def changes(f, carry):
        base = pl.multiple_of((f + 2) * STRIDE + LEAD, 8)
        value = padded[pl.ds(base, wide)] - 2.0 * term[pl.ds(base, wide)]
        for by, turn in shifts:
            code = float(4 * by + turn)
            value = value + gained(code_plus, base - by * STRIDE - turn, code)
            value = value + gained(code_minus, base + by * STRIDE + turn, code)
        out[pl.ds(f * NDIR, NDIR)] = value[:NDIR]
        return carry

    lax.fori_loop(0, NFREQ, changes, 0, unroll=4)
    high = (NFREQ + 1) * STRIDE + LEAD
    low = 2 * STRIDE + LEAD
    for turn in (1, 2, 3):
        code = float(4 + turn)
        out[BINS - NDIR :] = out[BINS - NDIR :] + gained(code_plus, high - turn, code)[:NDIR]
        out[:NDIR] = out[:NDIR] + gained(code_minus, low + turn, code)[:NDIR]

    for group in range(GROUPS):
        for step in range(STEPS):
            for row in range(BLOCKS):
                ghost_copy(group, step, row).wait_send()
                back_copy(group, step, row).wait_send()
        for shift in range(1, SPEC):
            spec_copy(group, shift).wait_send()


def direction_table():
    rows = np.arange(TROWS)
    values = []
    for start in (0, NDIR // 2):
        angle = ((rows + start) % NDIR) * (2.0 * math.pi / NDIR)
        values += [np.cos(angle), np.sin(angle)]
    return np.repeat(np.stack(values)[:, :, None], 128, axis=2).astype(np.float32)


def on_device(
    spectrum, normals, conn, send_nodes, step_weight, group_speed, dia_plus, dia_minus, dia_coeff
):
    vmem = pl.BlockSpec(memory_space=pltpu.VMEM)
    smem = pl.BlockSpec(memory_space=pltpu.SMEM)
    return pl.pallas_call(
        kernel,
        out_shape=jax.ShapeDtypeStruct((BINS, SLOT), f32),
        in_specs=[vmem, vmem, vmem, vmem, vmem, smem, vmem, vmem, vmem, vmem],
        out_specs=vmem,
        scratch_shapes=[
            pltpu.VMEM((GROUPS, SPEC, PAD, 128), f32),
            pltpu.VMEM((2 * PAD, OWN), bf16),
            pltpu.VMEM((GROUPS, PARTS, EXT), f8),
            pltpu.VMEM((OWN, BLOCKS * SLOT), bf16),
            pltpu.VMEM((EXT, 3 * ELEM), f8),
            pltpu.VMEM((EXT, 2 * ELEM), f8),
            pltpu.VMEM((6, TROWS, ELEM), f32),
            pltpu.VMEM((PARTS, 2 * CHUNK), f32),
            pltpu.VMEM((PARTS, 2 * CHUNK), f32),
            pltpu.VMEM((PARTS, 3 * CHUNK), f32),
            pltpu.VMEM((GROUPS, PARTS, 3 * ELEM), f8),
            pltpu.VMEM((GROUPS, PAD, OWN), f32),
            pltpu.VMEM((GROUPS, STEPS, BLOCKS, PAD, SLOT), f32),
            pltpu.VMEM((GROUPS, STEPS, BLOCKS, PAD, SLOT), f32),
            pltpu.VMEM((GROUPS, STEPS, BLOCKS, PAD, SLOT), f32),
            pltpu.VMEM((GROUPS, STEPS, BLOCKS, PAD, SLOT), f32),
            pltpu.VMEM((SPEC, ROWS + 6, 128), f32),
            pltpu.VMEM((BINS + 8, 128), f32),
            pltpu.VMEM((PADDED, 128), f32),
            pltpu.VMEM((PADDED, 128), f32),
            pltpu.VMEM((PADDED, 128), f32),
            pltpu.VMEM((PADDED, 128), f32),
            pltpu.VMEM((PADDED, 128), f32),
            pltpu.SemaphoreType.DMA((GROUPS, STEPS, 2, BLOCKS)),
            pltpu.SemaphoreType.DMA((GROUPS, STEPS, 2, BLOCKS)),
            pltpu.SemaphoreType.DMA((GROUPS, SPEC - 1)),
            pltpu.SemaphoreType.DMA((GROUPS, SPEC - 1)),
        ],
        compiler_params=pltpu.CompilerParams(
            collective_id=0, has_side_effects=True, vmem_limit_bytes=62 * 2**20
        ),
    )(
        spectrum,
        jnp.transpose(normals, (1, 0, 2)),
        conn,
        send_nodes,
        step_weight[None, :],
        group_speed,
        dia_plus,
        dia_minus,
        dia_coeff,
        jnp.asarray(direction_table()),
    )


def solution(mesh):
    in_specs = (
        P("spec", "dom"),
        P(None, None, "dom"),
        P(None, "dom"),
        P("dom", None, None),
        P("dom"),
        P(),
        P(),
        P(),
        P(),
    )
    out_specs = P(None, ("dom", "spec"))
    return jax.shard_map(
        on_device, mesh=mesh, in_specs=in_specs, out_specs=out_specs, check_vma=False
    )
```
